512 devices in a mesh: space: 64 (over z, x), coil: 8 (over y, core).
Axes of the slice: x: 4, y: 4, z: 16, core: 2. Of those that a mesh axis runs over, the one named last changes fastest.
Arguments:
- sample_values: bfloat16 [16, 2, 262144], P('coil', None, 'space'), may hold values from -6 to 6
- sample_offsets: bfloat16 [3, 262144], P(None, 'space'), may hold values from 0 to 1
- sample_cells: int32 [262144], P('space'), may hold values from 0 to 262143, as said below
- sample_slots: int32 [262144], P('space'), may hold values from 0 to 4096, as said below
- sensitivity: bfloat16 [16, 2, 256, 256, 256], P('coil', None, None, 'space'), may hold values from -5 to 5
Outputs:
- image: float32 [2, 256, 256, 256], P(None, 'coil', 'space')
The draws below stay inside these ranges and needn't reach their ends.
Inputs may be any that keep to these rules, and one draw needn't show every extreme that they name: Slots q * 64 to (q + 1) * 64 - 1 of each space index hold samples for space index q. sample_slots gives a used sample's place in q's buffer of 16 tiles of 256 slots: tile (sample_slots // 256) covers rows 16 times the tile number onward, and no two used samples for one destination share a place; the value 16 * 256 marks an unused slot. Some destination has all its places used, so it receives 64 samples from every space index. `sample_cells`: (x * 256 + y) * 256 + z with x the plane within the destination's 4 planes; for a used sample y // 16 equals sample_slots // 256.
All inputs are finite; a program needn't handle non-finite values.
Results may differ from the reference program's by a relative error of at most 0.006.
The reference program's roundings to bfloat16 on the way count: a program that leaves them out, or rounds other values in their place, can miss the bound.
Values may be sent and summed in bfloat16 or wider, within the bound.
No kernel may reach another device: no remote copies, remote signals or barrier semaphores. Data moves between devices by JAX's collectives and lax.ppermute only.
A program may use at most 128 MiB of HBM per device.

```python
import math
import jax
import jax.numpy as jnp
from jax import lax

GX = 256
GY = 256
GZ = 256
TY = 16
TCAP = 256
COILS = 16
SEND_DEV = 4096
CAP = 64
SAMPLES = 262144
N_SPACE = 64


def routing(key):
    tiles = GY // TY
    planes = GX // N_SPACE
    key_load, key_plane, key_row, key_depth, key_spare = jax.random.split(key, 5)
    loads = jax.random.randint(key_load, (N_SPACE, tiles), TCAP // 4, TCAP // 2 + 1, dtype=jnp.int32)
    loads = loads.at[N_SPACE // 2].set(TCAP)
    starts = (jnp.cumsum(loads, axis=1) - loads).astype(jnp.int32)
    ranks = jnp.arange(TCAP, dtype=jnp.int32)[None, None, :]
    filled = ranks < loads[:, :, None]
    order_index = starts[:, :, None] + ranks
    receiver = jnp.arange(N_SPACE, dtype=jnp.int32)[:, None, None]
    sender = (order_index + receiver) % N_SPACE
    position = order_index // N_SPACE
    overall = N_SPACE * SEND_DEV
    flat_target = jnp.where(filled, sender * SEND_DEV + receiver * CAP + position, overall).reshape(-1)
    tile_number = jnp.arange(tiles, dtype=jnp.int32)[None, :, None]
    grid_shape = (N_SPACE, tiles, TCAP)
    slot_value = jnp.broadcast_to(tile_number * TCAP + ranks, grid_shape).reshape(-1)
    plane_draw = jax.random.randint(key_plane, grid_shape, 0, planes, dtype=jnp.int32)
    row_draw = tile_number * TY + jax.random.randint(key_row, grid_shape, 0, TY, dtype=jnp.int32)
    depth_draw = jax.random.randint(key_depth, grid_shape, 0, GZ, dtype=jnp.int32)
    cell_value = ((plane_draw * GY + row_draw) * GZ + depth_draw).reshape(-1)
    first_spot = N_SPACE // 2 * tiles * TCAP
    last_spot = (N_SPACE // 2 * tiles + tiles - 1) * TCAP
    cell_value = cell_value.at[first_spot].set(0)
    cell_value = cell_value.at[last_spot].set(planes * GY * GZ - 1)
    slot_array = jnp.full((overall,), tiles * TCAP, jnp.int32).at[flat_target].set(slot_value, mode='drop')
    spare_cells = jax.random.randint(key_spare, (overall,), 0, planes * GY * GZ, dtype=jnp.int32)
    cell_array = spare_cells.at[flat_target].set(cell_value, mode='drop')
    return (cell_array, slot_array)


def draw_sample_cells(key, part):
    return routing(key)[0]


def draw_sample_slots(key, part):
    return routing(key)[1]


def block_scale(own_key, dims, shards, low, high):
    factor_of = 1.0
    for dim, blocks in shards:
        heights = jax.random.uniform(jax.random.fold_in(jax.random.fold_in(own_key, 6), dim), (blocks,), jnp.float32, low / len(shards), high / len(shards))
        factor_of = factor_of * jnp.repeat(jnp.exp(heights), dims[dim] // blocks).reshape((-1,) + (1,) * (len(dims) - 1 - dim))
    return factor_of


def centred(rng, extent, width, reach, shards=(), held_as=jnp.bfloat16):
    drawn = jax.random.normal(rng, extent, jnp.float32) * width
    if len(shards) > 0:
        drawn = block_scale(rng, extent, shards, -0.22, 0.18) * drawn
    return jnp.clip(drawn, min=-reach, max=reach).astype(held_as)


def setup_inputs(seed: int = 0) -> dict:
    seeds = jax.random.split(jax.random.key(seed), 6)
    sample_values = centred(seeds[0], (COILS, 2, SAMPLES), 1.0, 6.0, ((0, 8), (2, 64)))
    sample_offsets = jnp.clip(1.0 * jax.random.uniform(seeds[1], (3, SAMPLES), jnp.float32) ** block_scale(seeds[1], (3, SAMPLES), ((1, 64),), -0.2, 0.2), 0.0, 1.0).astype(jnp.bfloat16)
    sample_cells = draw_sample_cells(jax.random.fold_in(seeds[5], 71), 0)
    sample_slots = draw_sample_slots(jax.random.fold_in(seeds[5], 71), 0)
    sensitivity = centred(seeds[4], (COILS, 2, GX, GY, GZ), 0.7, 5.0, ((0, 8), (3, 64)))
    return dict(sample_values=sample_values, sample_offsets=sample_offsets, sample_cells=sample_cells, sample_slots=sample_slots, sensitivity=sensitivity)


BETA = 9.0

def bessel_zero(value):
    quarter = 0.25 * value * value
    term = jnp.ones_like(value)
    total = term
    for order in range(1, 31):
        term = term * quarter / float(order * order)
        total = total + term
    return total

def kaiser(distance):
    inner = jnp.maximum(1.0 - (0.5 * distance) ** 2, 0.0)
    return bessel_zero(BETA * jnp.sqrt(inner)) / bessel_zero(jnp.zeros((), jnp.float32) + BETA)

def tap_weights(fraction):
    shifts = jnp.arange(4, dtype=jnp.float32)
    return kaiser(fraction[None, :] + 1.0 - shifts[:, None])

def dft_table(length):
    counter = jnp.arange(length, dtype=jnp.int32)
    product = counter[:, None] * counter[None, :] % length
    phases = product.astype(jnp.float32) * (2.0 * math.pi / length)
    factor = 1.0 / math.sqrt(length)
    cosine = jnp.cos(phases) * factor
    sine = jnp.sin(phases) * factor
    return jnp.stack([jnp.stack([cosine, sine], 1), jnp.stack([-sine, cosine], 1)], 0).astype(jnp.bfloat16)

def weigh(images, maps):
    image_f = images.astype(jnp.float32)
    map_f = maps.astype(jnp.float32)
    real_part = lax.optimization_barrier(jnp.sum(map_f[:, 0] * image_f[:, 0] + map_f[:, 1] * image_f[:, 1], axis=0))
    imag_part = lax.optimization_barrier(jnp.sum(map_f[:, 0] * image_f[:, 1] - map_f[:, 1] * image_f[:, 0], axis=0))
    return jnp.stack([real_part, imag_part], 0)

def reference(sample_values, sample_offsets, sample_cells, sample_slots, sensitivity):
    send_dev = GY // TY * TCAP
    per_peer = send_dev // N_SPACE
    planes = GX // N_SPACE
    counter = jnp.arange(sample_cells.shape[0], dtype=jnp.int32)
    target = counter % send_dev // per_peer
    used = sample_slots < send_dev
    x_base = target * planes + sample_cells // (GY * GZ)
    y_base = sample_cells // GZ % GY
    z_base = sample_cells % GZ
    fraction = sample_offsets.astype(jnp.float32)
    weight_x = tap_weights(fraction[0])
    weight_y = tap_weights(fraction[1])
    weight_z = tap_weights(fraction[2]).astype(jnp.bfloat16)
    tap_steps = jnp.arange(4, dtype=jnp.int32)[:, None]
    x_cell = (x_base[None, :] + tap_steps - 1) % GX
    y_cell = (y_base[None, :] + tap_steps - 1) % GY
    z_cell = (z_base[None, :] + tap_steps - 1) % GZ
    flat_index = ((x_cell[:, None, None, :] * GY + y_cell[None, :, None, :]) * GZ + z_cell[None, None, :, :]).reshape(-1)
    z_table = dft_table(GZ).astype(jnp.float32)
    y_table = dft_table(GY).astype(jnp.float32)
    x_table = dft_table(GX).astype(jnp.float32)

    def one_coil(image_sum, inputs):
        coil_values, coil_maps = inputs
        kept = jnp.where(used[None, :], coil_values.astype(jnp.float32), jnp.zeros((), jnp.float32))
        pair = (kept[:, None, None, :] * weight_x[None, :, None, :] * weight_y[None, None, :, :]).astype(jnp.bfloat16)
        spread = pair[:, :, :, None, :].astype(jnp.float32) * weight_z[None, None, None, :, :].astype(jnp.float32)
        grid_sum = jnp.zeros((2, GX * GY * GZ), jnp.float32).at[:, flat_index].add(spread.reshape(2, -1))
        grid = grid_sum.reshape(2, GX, GY, GZ).astype(jnp.bfloat16)
        along_z = jnp.einsum('rxyz,rzsn->sxyn', grid.astype(jnp.float32), z_table).astype(jnp.bfloat16)
        along_y = jnp.einsum('rxyz,rysn->sxnz', along_z.astype(jnp.float32), y_table).astype(jnp.bfloat16)
        coil_image = jnp.einsum('rxyz,rxsn->snyz', along_y.astype(jnp.float32), x_table).astype(jnp.bfloat16)
        return (image_sum + weigh(coil_image[None], coil_maps[None]), None)
    image, _ = lax.scan(one_coil, jnp.zeros((2, GX, GY, GZ), jnp.float32), (sample_values, sensitivity))
    return image
```

```python
import math

import jax
import jax.numpy as jnp
import ml_dtypes
import numpy as np
from jax import lax
from jax.experimental import pallas as pl
from jax.experimental.pallas import tpu as pltpu
from jax.sharding import Mesh
from jax.sharding import PartitionSpec as P

GX = 256
GY = 256
GZ = 256
SLOTS = 4096
CAP = 64

BETA = 9.0
TERMS = 31

GROUPS = 8
BLOCKS = 8
ZN = 16
LANES = 256
STEP = 4
COILS = 4
ROWS = 16
TAPS = 4
SPAN = 7
PAIR = 2 * COILS * ROWS
HALO = 4


def series():
    quarter = 0.25 * BETA * BETA
    terms = [quarter**k / float(math.factorial(k)) ** 2 for k in range(TERMS)]
    total = math.fsum(terms)
    return [float(np.float32(t / total)) for t in terms]


def waves():
    counter = np.arange(256)
    phase = (counter[:, None] * counter[None, :] % 256).astype(np.float32) * np.float32(
        2.0 * math.pi / 256
    )
    scale = np.float32(1.0 / 16.0)
    both = np.stack([np.cos(phase) * scale, np.sin(phase) * scale], 0)
    return both.astype(ml_dtypes.bfloat16).astype(np.float32)


def z_table():
    cosine, sine = waves()
    return np.block([[cosine, sine], [-sine, cosine]]).astype(ml_dtypes.bfloat16)


def y_table():
    both = waves().reshape(2, ZN, ROWS, 256)
    return both.transpose(1, 0, 2, 3).reshape(ZN, 2 * ROWS, 256).astype(ml_dtypes.bfloat16)


def x_columns(planes, part):
    cosine, sine = waves()
    if part == 0:
        return np.concatenate([cosine[:, planes], sine[:, planes]], 0)
    return np.concatenate([-sine[:, planes], cosine[:, planes]], 0)


def x_tables():
    main = []
    for chunk in range(2):
        cols = []
        for group in range(GROUPS):
            planes = (32 * group + 16 * chunk + np.arange(16) - 1) % GX
            cols += [x_columns(planes, 0), x_columns(planes, 1)]
        main.append(np.concatenate(cols, 1))
    halo = []
    for coil in range(2):
        cols = []
        for group in range(GROUPS):
            planes = (32 * group + 32 + np.arange(HALO) - 1) % GX
            real = np.arange(HALO) < 3
            for other in range(2):
                keep = real & (other == coil)
                cols += [x_columns(planes, part) * keep for part in range(2)]
        halo.append(np.concatenate(cols, 1))
    return np.stack(main).astype(ml_dtypes.bfloat16), np.stack(halo).astype(ml_dtypes.bfloat16)


def tap_rows(first, second, lanes):
    row = lax.broadcasted_iota(jnp.int32, (8, lanes), 0)
    offset = jnp.where(row < TAPS, first, second)
    distance = offset + (1.0 - (row % TAPS).astype(jnp.float32))
    inner = jnp.maximum(1.0 - 0.25 * distance * distance, 0.0)
    coefficients = series()
    total = jnp.full((8, lanes), coefficients[-1], jnp.float32)
    for value in coefficients[-2::-1]:
        total = total * inner + value
    return total


def dense_rows(weights, base, lanes):
    high = base // 16
    low = base % 16
    row = lax.broadcasted_iota(jnp.int32, (16, lanes), 0)
    pattern = jnp.zeros((16, lanes), jnp.float32)
    for tap in range(TAPS):
        pattern = jnp.where(row == (low + tap) % 16, weights[tap], pattern)
    place = jnp.where(row < low, (high + 1) % 16, high).astype(jnp.float32)
    pattern = pattern.astype(jnp.bfloat16)
    place = place.astype(jnp.bfloat16)
    zero = jnp.zeros((16, lanes), jnp.bfloat16)
    return [
        jnp.where(place == jnp.bfloat16(block), pattern, zero) for block in range(16)
    ]


def build(packed, y_tab, pair_ref, dense_ref, at, lanes):
    taps_xy = tap_rows(packed[4:5], packed[5:6], lanes)
    taps_z = tap_rows(packed[6:7], packed[6:7], lanes)
    cell = packed.astype(jnp.int32)
    base_x = cell[12:13]
    base_y = (cell[13:14] + 255) % 256
    base_z = (cell[14:15] + 255) % 256
    z_blocks = dense_rows([taps_z[t : t + 1] for t in range(TAPS)], base_z, lanes)
    for block in range(16):
        dense_ref[block * 16 : (block + 1) * 16, at : at + lanes] = z_blocks[block]
    y_blocks = dense_rows([taps_xy[4 + t : 5 + t] for t in range(TAPS)], base_y, lanes)
    turn = jnp.dot(y_tab, jnp.concatenate(y_blocks, 0), preferred_element_type=jnp.float32)
    turn_re, turn_im = turn[:ROWS], turn[ROWS:]
    real, imag = [], []
    for coil in range(COILS):
        row = (coil // 2) * 8 + (coil % 2) * 2
        value_re, value_im = packed[row : row + 1], packed[row + 1 : row + 2]
        real.append((value_re * turn_re - value_im * turn_im).astype(jnp.bfloat16))
        imag.append((value_re * turn_im + value_im * turn_re).astype(jnp.bfloat16))
    values = real + imag
    row = lax.broadcasted_iota(jnp.int32, (8, lanes), 0)
    dense_x = jnp.zeros((8, lanes), jnp.float32)
    for tap in range(TAPS):
        dense_x = jnp.where(row == base_x + tap, taps_xy[tap : tap + 1], dense_x)
    for plane in range(SPAN):
        weight = jnp.broadcast_to(dense_x[plane : plane + 1], (ROWS, lanes)).astype(jnp.bfloat16)
        for part in range(2 * COILS):
            start = plane * PAIR + part * ROWS
            pair_ref[start : start + ROWS, at : at + lanes] = values[part] * weight


def emit(grid_planes, z_tab, flat):
    planes = grid_planes.shape[0]
    half = PAIR // 2
    grid = grid_planes.astype(jnp.bfloat16)
    joined = jnp.concatenate([grid[:, :half], grid[:, half:]], axis=2)
    along = jnp.dot(
        joined.reshape(planes * half, 2 * GZ), z_tab, preferred_element_type=jnp.float32
    )
    return jnp.swapaxes(along.reshape(planes, half, 2 * GZ), 0, 1)


def grid_kernel(blocks, samples_ref, y_ref, z_ref, carry_ref, main_ref, last_ref, pair_ref, dense_ref, acc_ref):
    q = pl.program_id(0)
    planes = 4 * blocks

    @pl.when(q == 0)
    def _():
        acc_ref[0:HALO] = carry_ref[...]
        acc_ref[HALO:] = jnp.zeros((planes, PAIR, GZ), jnp.float32)

    y_tab = y_ref[...]

    def step(index, _):
        for part in range(STEP):
            packed = samples_ref[index * STEP + part, 0].astype(jnp.float32)
            build(packed, y_tab, pair_ref, dense_ref, part * LANES, LANES)
        product = lax.dot_general(
            pair_ref[...], dense_ref[...], (((1,), (1,)), ((), ())), preferred_element_type=jnp.float32
        )
        here = pl.ds(4 * q, SPAN)
        acc_ref[here] = acc_ref[here] + product.reshape(SPAN, PAIR, GZ)
        return 0

    lax.fori_loop(0, ZN // STEP, step, 0)

    @pl.when(q == blocks - 1)
    def _():
        z_tab = z_ref[...]
        out = emit(acc_ref[0:planes], z_tab, None).astype(jnp.bfloat16)
        for coil in range(COILS):
            for row in range(ROWS):
                line = out[coil * ROWS + row]
                for part in range(2):
                    main_ref[
                        (row // 4) * 2 + coil // 2,
                        coil % 2,
                        part,
                        :,
                        (row % 4) * GZ : (row % 4 + 1) * GZ,
                    ] = line[:, part * GZ : (part + 1) * GZ]
        last_ref[...] = acc_ref[planes:]


def grid_chunk(samples, y_tab, z_tab, carry):
    blocks = samples.shape[1]
    planes = 4 * blocks
    return pl.pallas_call(
        lambda *refs: grid_kernel(blocks, *refs),
        grid=(blocks,),
        in_specs=[
            pl.BlockSpec((ZN, 1, 16, LANES), lambda q: (0, q, 0, 0)),
            pl.BlockSpec((2 * ROWS, GY), lambda q: (0, 0)),
            pl.BlockSpec((2 * GZ, 2 * GZ), lambda q: (0, 0)),
            pl.BlockSpec((HALO, PAIR, GZ), lambda q: (0, 0, 0)),
        ],
        out_specs=[
            pl.BlockSpec((GROUPS, 2, 2, planes, 4 * GZ), lambda q: (0, 0, 0, 0, 0)),
            pl.BlockSpec((HALO, PAIR, GZ), lambda q: (0, 0, 0)),
        ],
        out_shape=[
            jax.ShapeDtypeStruct((GROUPS, 2, 2, planes, 4 * GZ), jnp.bfloat16),
            jax.ShapeDtypeStruct((HALO, PAIR, GZ), jnp.float32),
        ],
        scratch_shapes=[
            pltpu.VMEM((SPAN * PAIR, STEP * LANES), jnp.bfloat16),
            pltpu.VMEM((GZ, STEP * LANES), jnp.bfloat16),
            pltpu.VMEM((planes + HALO, PAIR, GZ), jnp.float32),
        ],
        compiler_params=pltpu.CompilerParams(vmem_limit_bytes=48 * 2**20),
        name="grid_chunk",
    )(samples, y_tab, z_tab, carry)


def halo_kernel(last_ref, z_ref, out_ref):
    rows = emit(last_ref[...], z_ref[...], None)
    for coil in range(0, COILS, 2):
        for row in range(ROWS):
            pieces = []
            for inner in range(2):
                line = rows[(coil + inner) * ROWS + row]
                pieces += [line[:, :GZ], line[:, GZ:]]
            out_ref[(row // 4) * 2 + coil // 2, :, (row % 4) * GZ : (row % 4 + 1) * GZ] = (
                jnp.concatenate(pieces, 0).astype(jnp.bfloat16)
            )


def halo_rows(last, z_tab):
    return pl.pallas_call(
        halo_kernel,
        out_shape=jax.ShapeDtypeStruct((GROUPS, 16, 4 * GZ), jnp.bfloat16),
        compiler_params=pltpu.CompilerParams(vmem_limit_bytes=32 * 2**20),
        name="halo_rows",
    )(last, z_tab)


def combine_kernel(first_ref, second_ref, halo_ref, main_ref, edge_ref, maps_ref, out_ref):
    total = [None, None]
    edge_rows = halo_ref[...].reshape(GROUPS * 16, GZ)
    for coil in range(2):
        image = jnp.dot(
            edge_ref[coil], edge_rows, preferred_element_type=jnp.float32
        )
        for chunk, ref in enumerate((first_ref, second_ref)):
            rows = ref[:, coil].reshape(GROUPS * 32, GZ)
            image = image + jnp.dot(main_ref[chunk], rows, preferred_element_type=jnp.float32)
        image_re, image_im = image[:GX], image[GX:]
        map_re = maps_ref[coil, 0].astype(jnp.float32)
        map_im = maps_ref[coil, 1].astype(jnp.float32)
        real = map_re * image_re + map_im * image_im
        imag = map_re * image_im - map_im * image_re
        total = [real, imag] if coil == 0 else [total[0] + real, total[1] + imag]
    out_ref[0] = total[0].astype(out_ref.dtype)
    out_ref[1] = total[1].astype(out_ref.dtype)


def combine(first, second, halo, maps, dtype):
    main_tab, edge_tab = x_tables()
    return pl.pallas_call(
        combine_kernel,
        grid=(4,),
        in_specs=[
            pl.BlockSpec((GROUPS, 2, 2, 16, GZ), lambda y: (0, 0, 0, 0, y)),
            pl.BlockSpec((GROUPS, 2, 2, 16, GZ), lambda y: (0, 0, 0, 0, y)),
            pl.BlockSpec((GROUPS, 16, GZ), lambda y: (0, 0, y)),
            pl.BlockSpec((2, 2 * GX, GROUPS * 32), lambda y: (0, 0, 0)),
            pl.BlockSpec((2, 2 * GX, GROUPS * 16), lambda y: (0, 0, 0)),
            pl.BlockSpec((2, 2, GX, GZ), lambda y: (0, 0, 0, y)),
        ],
        out_specs=pl.BlockSpec((2, GX, GZ), lambda y: (0, 0, y)),
        out_shape=jax.ShapeDtypeStruct((2, GX, 4 * GZ), dtype),
        compiler_params=pltpu.CompilerParams(vmem_limit_bytes=48 * 2**20),
        name="combine",
    )(first, second, halo, jnp.asarray(main_tab), jnp.asarray(edge_tab), maps)


def pack(values, offsets, cells, slots):
    used = slots < SLOTS
    kept = jnp.where(used[None, :], values.reshape(4, SLOTS), jnp.zeros((), jnp.bfloat16))
    spots = jnp.stack([cells // (GY * GZ), cells // GZ % GY, cells % GZ], 0).astype(jnp.bfloat16)
    about = jnp.where(lax.axis_index("core") == 0, offsets, spots)
    rows = jnp.concatenate([kept, about, jnp.zeros((1, SLOTS), jnp.bfloat16)], 0)
    return rows.reshape(8, GROUPS, BLOCKS * CAP).swapaxes(0, 1)


def body(sample_values, sample_offsets, sample_cells, sample_slots, sensitivity):
    packed = pack(sample_values, sample_offsets, sample_cells, sample_slots)
    got = lax.all_to_all(packed, ("x", "core"), split_axis=0, concat_axis=0, tiled=True)
    got = got.reshape(4, 2, 8, BLOCKS, CAP).transpose(3, 1, 2, 0, 4).reshape(BLOCKS, 16, LANES)
    samples = lax.all_gather(got, "z", axis=0, tiled=False)
    y_tab = lax.dynamic_index_in_dim(jnp.asarray(y_table()), lax.axis_index("z"), 0, keepdims=False)
    z_tab = jnp.asarray(z_table())
    carry = jnp.zeros((HALO, PAIR, GZ), jnp.float32)
    parts = []
    for chunk in range(2):
        part, carry = grid_chunk(samples[:, 4 * chunk : 4 * chunk + 4], y_tab, z_tab, carry)
        parts.append(part)
    halo = halo_rows(carry, z_tab)
    turned = [
        lax.all_to_all(part, ("x", "core"), split_axis=0, concat_axis=0, tiled=True)
        for part in parts + [halo]
    ]
    maps = sensitivity.reshape(2, 2, GX, 4 * GZ)
    partial = combine(*turned, maps, jnp.float32)
    image = lax.psum_scatter(partial, ("y", "core"), scatter_dimension=1, tiled=True)
    return image.reshape(2, GX // 8, 4, GZ)


def solution(mesh):
    fine = Mesh(mesh.devices.reshape(16, 4, 4, 2), ("z", "x", "y", "core"))
    space, coil = ("z", "x"), ("y", "core")
    placed = (
        P(coil, None, space),
        P(None, space),
        P(space),
        P(space),
        P(coil, None, None, space, None),
    )
    return jax.shard_map(
        body, mesh=fine, in_specs=placed, out_specs=P(None, coil, space, None), check_vma=False
    )
```

```python
import math

import jax
import jax.numpy as jnp
import ml_dtypes
import numpy as np
from jax import lax
from jax.experimental import pallas as pl
from jax.experimental.pallas import tpu as pltpu
from jax.sharding import Mesh
from jax.sharding import PartitionSpec as P

GX = 256
GY = 256
GZ = 256
SLOTS = 4096
CAP = 64

BETA = 9.0
TERMS = 31

ZH = 8
GROUPS = 16
BLOCKS = 4
CHUNKS = 2
LANES = 512
STEP = 2
COILS = 4
ROWS = 32
TAPS = 4
SPAN = 7
PAIR = 2 * COILS * ROWS
HALF = PAIR // 2
PLANES = 8
HALO = 4


def series():
    quarter = 0.25 * BETA * BETA
    terms = [quarter**k / float(math.factorial(k)) ** 2 for k in range(TERMS)]
    total = math.fsum(terms)
    return [float(np.float32(t / total)) for t in terms]


def waves():
    counter = np.arange(256)
    phase = (counter[:, None] * counter[None, :] % 256).astype(np.float32) * np.float32(
        2.0 * math.pi / 256
    )
    scale = np.float32(1.0 / 16.0)
    both = np.stack([np.cos(phase) * scale, np.sin(phase) * scale], 0)
    return both.astype(ml_dtypes.bfloat16).astype(np.float32)


def z_table():
    cosine, sine = waves()
    return np.block([[cosine, sine], [-sine, cosine]]).astype(ml_dtypes.bfloat16)


def y_table():
    both = waves().reshape(2, ZH, ROWS, 256)
    return both.transpose(1, 0, 2, 3).reshape(ZH, 2 * ROWS, 256).astype(ml_dtypes.bfloat16)


def x_columns(planes, part):
    cosine, sine = waves()
    if part == 0:
        return np.concatenate([cosine[:, planes], sine[:, planes]], 0)
    return np.concatenate([-sine[:, planes], cosine[:, planes]], 0)


def x_tables():
    main = []
    for chunk in range(CHUNKS):
        cols = []
        for group in range(GROUPS):
            planes = (16 * group + PLANES * chunk + np.arange(PLANES) - 1) % GX
            cols += [x_columns(planes, 0), x_columns(planes, 1)]
        main.append(np.concatenate(cols, 1))
    halo = []
    for coil in range(2):
        cols = []
        for group in range(GROUPS):
            planes = (16 * group + 16 + np.arange(HALO) - 1) % GX
            real = np.arange(HALO) < 3
            for other in range(2):
                keep = real & (other == coil)
                cols += [x_columns(planes, part) * keep for part in range(2)]
        halo.append(np.concatenate(cols, 1))
    return np.stack(main).astype(ml_dtypes.bfloat16), np.stack(halo).astype(ml_dtypes.bfloat16)


def tap_rows(first, second, lanes):
    row = lax.broadcasted_iota(jnp.int32, (8, lanes), 0)
    offset = jnp.where(row < TAPS, first, second)
    distance = offset + (1.0 - (row % TAPS).astype(jnp.float32))
    inner = jnp.maximum(1.0 - 0.25 * distance * distance, 0.0)
    coefficients = series()
    total = jnp.full((8, lanes), coefficients[-1], jnp.float32)
    for value in coefficients[-2::-1]:
        total = total * inner + value
    return total


def dense_rows(weights, base, lanes):
    high = base // 16
    low = base % 16
    row = lax.broadcasted_iota(jnp.int32, (16, lanes), 0)
    pattern = jnp.zeros((16, lanes), jnp.float32)
    for tap in range(TAPS):
        pattern = jnp.where(row == (low + tap) % 16, weights[tap], pattern)
    place = jnp.where(row < low, (high + 1) % 16, high).astype(jnp.float32)
    pattern = pattern.astype(jnp.bfloat16)
    place = place.astype(jnp.bfloat16)
    zero = jnp.zeros((16, lanes), jnp.bfloat16)
    return [
        jnp.where(place == jnp.bfloat16(block), pattern, zero) for block in range(16)
    ]


def build(packed, y_tab, pair_ref, dense_ref, at, lanes):
    taps_xy = tap_rows(packed[4:5], packed[5:6], lanes)
    taps_z = tap_rows(packed[6:7], packed[6:7], lanes)
    cell = packed.astype(jnp.int32)
    base_x = cell[12:13]
    base_y = (cell[13:14] + 255) % 256
    base_z = (cell[14:15] + 255) % 256
    z_blocks = dense_rows([taps_z[t : t + 1] for t in range(TAPS)], base_z, lanes)
    for block in range(16):
        dense_ref[block * 16 : (block + 1) * 16, at : at + lanes] = z_blocks[block]
    y_blocks = dense_rows([taps_xy[4 + t : 5 + t] for t in range(TAPS)], base_y, lanes)
    turn = jnp.dot(y_tab, jnp.concatenate(y_blocks, 0), preferred_element_type=jnp.float32)
    turn_re, turn_im = turn[:ROWS], turn[ROWS:]
    real, imag = [], []
    for coil in range(COILS):
        row = (coil // 2) * 8 + (coil % 2) * 2
        value_re, value_im = packed[row : row + 1], packed[row + 1 : row + 2]
        real.append((value_re * turn_re - value_im * turn_im).astype(jnp.bfloat16))
        imag.append((value_re * turn_im + value_im * turn_re).astype(jnp.bfloat16))
    values = real + imag
    row = lax.broadcasted_iota(jnp.int32, (8, lanes), 0)
    dense_x = jnp.zeros((8, lanes), jnp.float32)
    for tap in range(TAPS):
        dense_x = jnp.where(row == base_x + tap, taps_xy[tap : tap + 1], dense_x)
    for plane in range(SPAN):
        weight = jnp.broadcast_to(dense_x[plane : plane + 1], (ROWS, lanes)).astype(jnp.bfloat16)
        for part in range(2 * COILS):
            start = plane * PAIR + part * ROWS
            pair_ref[start : start + ROWS, at : at + lanes] = values[part] * weight


def transform_z(grid_planes, z_tab):
    planes = grid_planes.shape[0]
    grid = grid_planes.astype(jnp.bfloat16)
    joined = jnp.concatenate([grid[:, :HALF], grid[:, HALF:]], axis=2)
    along = jnp.dot(
        joined.reshape(planes * HALF, 2 * GZ), z_tab, preferred_element_type=jnp.float32
    )
    return jnp.swapaxes(along.reshape(planes, HALF, 2 * GZ), 0, 1)


def grid_kernel(last, samples_ref, y_ref, z_ref, carry_ref, out_ref, carried_ref, pair_ref, dense_ref, acc_ref):
    q = pl.program_id(0)

    @pl.when(q == 0)
    def _():
        acc_ref[0:HALO] = carry_ref[...]
        acc_ref[HALO:] = jnp.zeros((PLANES, PAIR, GZ), jnp.float32)

    y_tab = y_ref[...]

    def step(index, _):
        for part in range(STEP):
            packed = samples_ref[index * STEP + part, 0].astype(jnp.float32)
            build(packed, y_tab, pair_ref, dense_ref, part * LANES, LANES)
        product = lax.dot_general(
            pair_ref[...], dense_ref[...], (((1,), (1,)), ((), ())), preferred_element_type=jnp.float32
        )
        here = pl.ds(4 * q, SPAN)
        acc_ref[here] = acc_ref[here] + product.reshape(SPAN, PAIR, GZ)
        return 0

    lax.fori_loop(0, ZH // STEP, step, 0)

    @pl.when(q == BLOCKS // CHUNKS - 1)
    def _():
        z_tab = z_ref[...]
        lines = transform_z(acc_ref[0:PLANES], z_tab)
        for coil in range(COILS):
            for row in range(ROWS):
                line = lines[coil * ROWS + row]
                both = jnp.concatenate([line[:, :GZ], line[:, GZ:]], 0).astype(jnp.bfloat16)
                out_ref[
                    (row // 4) * 2 + coil // 2, coil % 2, :, (row % 4) * GZ : (row % 4 + 1) * GZ
                ] = both
        if last:
            edge = transform_z(acc_ref[PLANES:], z_tab)
            for coil in range(0, COILS, 2):
                for row in range(ROWS):
                    pieces = []
                    for inner in range(2):
                        line = edge[(coil + inner) * ROWS + row]
                        pieces += [line[:, :GZ], line[:, GZ:]]
                    out_ref[
                        (row // 4) * 2 + coil // 2, 2, :, (row % 4) * GZ : (row % 4 + 1) * GZ
                    ] = jnp.concatenate(pieces, 0).astype(jnp.bfloat16)
        else:
            carried_ref[...] = acc_ref[PLANES:]


def grid_chunk(samples, y_tab, z_tab, carry, chunk):
    blocks = BLOCKS // CHUNKS
    last = chunk == CHUNKS - 1
    tiles = 3 if last else 2
    flops = 2 * SPAN * PAIR * GZ * ZH * LANES * blocks + 2 * PLANES * PAIR * GZ * 2 * GZ
    return pl.pallas_call(
        lambda *refs: grid_kernel(last, *refs),
        grid=(blocks,),
        in_specs=[
            pl.BlockSpec((ZH, 1, 16, LANES), lambda q: (0, q + chunk * blocks, 0, 0)),
            pl.BlockSpec((2 * ROWS, GY), lambda q: (0, 0)),
            pl.BlockSpec((2 * GZ, 2 * GZ), lambda q: (0, 0)),
            pl.BlockSpec((HALO, PAIR, GZ), lambda q: (0, 0, 0)),
        ],
        out_specs=[
            pl.BlockSpec((GROUPS, tiles, 16, 4 * GZ), lambda q: (0, 0, 0, 0)),
            pl.BlockSpec((HALO, PAIR, GZ), lambda q: (0, 0, 0)),
        ],
        out_shape=[
            jax.ShapeDtypeStruct((GROUPS, tiles, 16, 4 * GZ), jnp.bfloat16),
            jax.ShapeDtypeStruct((HALO, PAIR, GZ), jnp.float32),
        ],
        scratch_shapes=[
            pltpu.VMEM((SPAN * PAIR, STEP * LANES), jnp.bfloat16),
            pltpu.VMEM((GZ, STEP * LANES), jnp.bfloat16),
            pltpu.VMEM((PLANES + HALO, PAIR, GZ), jnp.float32),
        ],
        compiler_params=pltpu.CompilerParams(vmem_limit_bytes=48 * 2**20),
        cost_estimate=pl.CostEstimate(
            flops=flops, bytes_accessed=4 * 2**20, transcendentals=0
        ),
        name="grid_chunk",
    )(samples, y_tab, z_tab, carry)


def combine_kernel(first_ref, second_ref, main_ref, edge_ref, maps_ref, out_ref):
    total = [None, None]
    depth = GROUPS * 16
    edge_rows = second_ref[:, 2].reshape(depth, GZ)
    for coil in range(2):
        image = jnp.dot(edge_ref[coil], edge_rows, preferred_element_type=jnp.float32)
        for chunk, ref in enumerate((first_ref, second_ref)):
            rows = ref[:, coil].reshape(depth, GZ)
            image = image + jnp.dot(main_ref[chunk], rows, preferred_element_type=jnp.float32)
        image_re, image_im = image[:GX], image[GX:]
        map_re = maps_ref[coil, 0].astype(jnp.float32)
        map_im = maps_ref[coil, 1].astype(jnp.float32)
        real = map_re * image_re + map_im * image_im
        imag = map_re * image_im - map_im * image_re
        total = [real, imag] if coil == 0 else [total[0] + real, total[1] + imag]
    for part in range(2):
        out_ref[:, part] = total[part].astype(jnp.bfloat16).reshape(8, GX // 8, GZ)


def combine(first, second, maps):
    main_tab, edge_tab = x_tables()
    depth = GROUPS * 16
    return pl.pallas_call(
        combine_kernel,
        grid=(4,),
        in_specs=[
            pl.BlockSpec((GROUPS, 2, 16, GZ), lambda y: (0, 0, 0, y)),
            pl.BlockSpec((GROUPS, 3, 16, GZ), lambda y: (0, 0, 0, y)),
            pl.BlockSpec((CHUNKS, 2 * GX, depth), lambda y: (0, 0, 0)),
            pl.BlockSpec((2, 2 * GX, depth), lambda y: (0, 0, 0)),
            pl.BlockSpec((2, 2, GX, GZ), lambda y: (0, 0, 0, y)),
        ],
        out_specs=pl.BlockSpec((8, 2, GX // 8, GZ), lambda y: (0, 0, 0, y)),
        out_shape=jax.ShapeDtypeStruct((8, 2, GX // 8, 4 * GZ), jnp.bfloat16),
        compiler_params=pltpu.CompilerParams(vmem_limit_bytes=48 * 2**20),
        cost_estimate=pl.CostEstimate(
            flops=2 * 2 * 2 * GX * 3 * depth * 4 * GZ, bytes_accessed=8 * 2**20, transcendentals=0
        ),
        name="combine",
    )(first, second, jnp.asarray(main_tab), jnp.asarray(edge_tab), maps)


def pack(values, offsets, cells, slots):
    used = slots < SLOTS
    kept = jnp.where(used[None, :], values.reshape(4, SLOTS), jnp.zeros((), jnp.bfloat16))
    spots = jnp.stack([cells // (GY * GZ), cells // GZ % GY, cells % GZ], 0).astype(jnp.bfloat16)
    about = jnp.where(lax.axis_index("core") == 0, offsets, spots)
    rows = jnp.concatenate([kept, about, jnp.zeros((1, SLOTS), jnp.bfloat16)], 0)
    return rows.reshape(8, GROUPS, BLOCKS * CAP).swapaxes(0, 1)


def turn(array, axes):
    return lax.all_to_all(array, axes, split_axis=0, concat_axis=0, tiled=True)


def body(sample_values, sample_offsets, sample_cells, sample_slots, sensitivity):
    packed = pack(sample_values, sample_offsets, sample_cells, sample_slots)
    planes = ("zl", "x", "core")
    got = turn(packed, planes)
    got = got.reshape(8, 2, 8, BLOCKS, CAP).transpose(3, 1, 2, 0, 4).reshape(BLOCKS, 16, LANES)
    samples = turn(jnp.broadcast_to(got[None], (ZH,) + got.shape), "zh")
    y_tab = lax.dynamic_index_in_dim(
        jnp.asarray(y_table()), lax.axis_index("zh"), 0, keepdims=False
    )
    z_tab = jnp.asarray(z_table())
    carry = jnp.zeros((HALO, PAIR, GZ), jnp.float32)
    turned = []
    for chunk in range(CHUNKS):
        part, carry = grid_chunk(samples, y_tab, z_tab, carry, chunk)
        turned.append(turn(part, planes))
    maps = sensitivity.reshape(2, 2, GX, 4 * GZ)
    partial = turn(combine(*turned, maps), ("y", "core"))
    image = jnp.sum(partial.astype(jnp.float32), axis=0)
    return image.reshape(2, GX // 8, 4, GZ)


def solution(mesh):
    fine = Mesh(mesh.devices.reshape(8, 2, 4, 4, 2), ("zh", "zl", "x", "y", "core"))
    space, coil = ("zh", "zl", "x"), ("y", "core")
    placed = (
        P(coil, None, space),
        P(None, space),
        P(space),
        P(space),
        P(coil, None, None, space, None),
    )
    return jax.shard_map(
        body, mesh=fine, in_specs=placed, out_specs=P(None, coil, space, None), check_vma=False
    )
```

```python
import math

import jax
import jax.numpy as jnp
import ml_dtypes
import numpy as np
from jax import lax
from jax.experimental import pallas as pl
from jax.experimental.pallas import tpu as pltpu
from jax.sharding import Mesh
from jax.sharding import PartitionSpec as P

GX = 256
GY = 256
GZ = 256
SLOTS = 4096
CAP = 64

BETA = 9.0
TERMS = 31

ZH = 8
GROUPS = 16
BLOCKS = 4
CHUNKS = 2
QS = BLOCKS // CHUNKS
SOURCES = 64
LANES = 512
STEP = 2
COILS = 4
ROWS = 32
TAPS = 4
SPAN = 7
PLANES = 4 * QS
HALO = 4


def series():
    quarter = 0.25 * BETA * BETA
    terms = [quarter**k / float(math.factorial(k)) ** 2 for k in range(TERMS)]
    total = math.fsum(terms)
    return [float(np.float32(t / total)) for t in terms]


def waves():
    counter = np.arange(256)
    phase = (counter[:, None] * counter[None, :] % 256).astype(np.float32) * np.float32(
        2.0 * math.pi / 256
    )
    scale = np.float32(1.0 / 16.0)
    both = np.stack([np.cos(phase) * scale, np.sin(phase) * scale], 0)
    return both.astype(ml_dtypes.bfloat16).astype(np.float32)


def z_table():
    cosine, sine = waves()
    return np.block([[cosine, sine], [-sine, cosine]]).astype(ml_dtypes.bfloat16)


def row_order(part):
    rows = [4 * owner + 2 * half + e for half in range(2) for owner in range(8) for e in range(2)]
    return rows if part is None else rows[16 * part : 16 * part + 16]


def y_table(part):
    both = waves().reshape(2, ZH, ROWS, 256)[:, :, row_order(part)]
    return both.transpose(1, 0, 2, 3).reshape(ZH, -1, 256).astype(ml_dtypes.bfloat16)


def x_columns(planes, part):
    cosine, sine = waves()
    if part == 0:
        return np.concatenate([cosine[:, planes], sine[:, planes]], 0)
    return np.concatenate([-sine[:, planes], cosine[:, planes]], 0)


def x_tables():
    main = []
    for chunk in range(CHUNKS):
        cols = []
        for group in range(GROUPS):
            planes = (16 * group + PLANES * chunk + np.arange(PLANES) - 1) % GX
            cols += [x_columns(planes, 0), x_columns(planes, 1)]
        main.append(np.concatenate(cols, 1))
    halo = []
    for coil in range(2):
        cols = []
        for group in range(GROUPS):
            planes = (16 * group + 16 + np.arange(HALO) - 1) % GX
            real = np.arange(HALO) < 3
            for other in range(2):
                keep = real & (other == coil)
                cols += [x_columns(planes, part) * keep for part in range(2)]
        halo.append(np.concatenate(cols, 1))
    return np.stack(main).astype(ml_dtypes.bfloat16), np.stack(halo).astype(ml_dtypes.bfloat16)


def tap_rows(first, second, lanes):
    row = lax.broadcasted_iota(jnp.int32, (8, lanes), 0)
    offset = jnp.where(row < TAPS, first, second)
    distance = offset + (1.0 - (row % TAPS).astype(jnp.float32))
    inner = jnp.maximum(1.0 - 0.25 * distance * distance, 0.0)
    coefficients = series()
    total = jnp.full((8, lanes), coefficients[-1], jnp.float32)
    for value in coefficients[-2::-1]:
        total = total * inner + value
    return total


def dense_rows(weights, base, lanes):
    high = base // 16
    low = base % 16
    row = lax.broadcasted_iota(jnp.int32, (16, lanes), 0)
    pattern = jnp.zeros((16, lanes), jnp.float32)
    for tap in range(TAPS):
        pattern = jnp.where(row == (low + tap) % 16, weights[tap], pattern)
    place = jnp.where(row < low, (high + 1) % 16, high).astype(jnp.float32)
    pattern = pattern.astype(jnp.bfloat16)
    place = place.astype(jnp.bfloat16)
    zero = jnp.zeros((16, lanes), jnp.bfloat16)
    return [
        jnp.where(place == jnp.bfloat16(block), pattern, zero) for block in range(16)
    ]


def gather(samples_ref, start, q):
    lane = lax.broadcasted_iota(jnp.int32, (16, 2 * CAP), 1)
    pieces = []
    for pair in range(LANES // (2 * CAP)):
        first = samples_ref[start + 2 * pair].astype(jnp.float32)
        second = samples_ref[start + 2 * pair + 1].astype(jnp.float32)
        first = jnp.where(q == 0, first, pltpu.roll(first, CAP, 1))
        second = jnp.where(q == 0, pltpu.roll(second, CAP, 1), second)
        pieces.append(jnp.where(lane < CAP, first, second))
    return jnp.concatenate(pieces, 1)


def build(packed, y_tab, pair_ref, dense_ref, at, lanes):
    rows = y_tab.shape[0] // 2
    taps_xy = tap_rows(packed[4:5], packed[5:6], lanes)
    taps_z = tap_rows(packed[6:7], packed[6:7], lanes)
    cell = packed.astype(jnp.int32)
    base_x = cell[12:13]
    base_y = (cell[13:14] + 255) % 256
    base_z = (cell[14:15] + 255) % 256
    z_blocks = dense_rows([taps_z[t : t + 1] for t in range(TAPS)], base_z, lanes)
    for block in range(16):
        dense_ref[block * 16 : (block + 1) * 16, at : at + lanes] = z_blocks[block]
    y_blocks = dense_rows([taps_xy[4 + t : 5 + t] for t in range(TAPS)], base_y, lanes)
    turn = jnp.dot(y_tab, jnp.concatenate(y_blocks, 0), preferred_element_type=jnp.float32)
    turn_re, turn_im = turn[:rows], turn[rows:]
    real, imag = [], []
    for coil in range(COILS):
        row = (coil // 2) * 8 + (coil % 2) * 2
        value_re, value_im = packed[row : row + 1], packed[row + 1 : row + 2]
        real.append((value_re * turn_re - value_im * turn_im).astype(jnp.bfloat16))
        imag.append((value_re * turn_im + value_im * turn_re).astype(jnp.bfloat16))
    values = real + imag
    row = lax.broadcasted_iota(jnp.int32, (8, lanes), 0)
    dense_x = jnp.zeros((8, lanes), jnp.float32)
    for tap in range(TAPS):
        dense_x = jnp.where(row == base_x + tap, taps_xy[tap : tap + 1], dense_x)
    for plane in range(SPAN):
        weight = jnp.broadcast_to(dense_x[plane : plane + 1], (rows, lanes)).astype(jnp.bfloat16)
        for part in range(2 * COILS):
            start = (plane * 2 * COILS + part) * rows
            pair_ref[start : start + rows, at : at + lanes] = values[part] * weight


def transform_z(grid_planes, z_tab):
    planes, _, rows, _ = grid_planes.shape
    half = COILS * rows
    grid = grid_planes.astype(jnp.bfloat16)
    joined = jnp.concatenate(
        [
            grid[:, :COILS].reshape(planes * half, GZ),
            grid[:, COILS:].reshape(planes * half, GZ),
        ],
        axis=1,
    )
    along = jnp.dot(joined, z_tab, preferred_element_type=jnp.float32)
    return jnp.swapaxes(along.reshape(planes, half, 2 * GZ), 0, 1)


def grid_kernel(last, samples_ref, y_ref, z_ref, *refs):
    if last:
        carry_ref, out_ref, pair_ref, dense_ref, acc_ref = refs
    else:
        out_ref, carried_ref, pair_ref, dense_ref, acc_ref = refs
    q = pl.program_id(0)
    rows = y_ref.shape[0] // 2

    @pl.when(q == 0)
    def _():
        if last:
            acc_ref[0:HALO] = carry_ref[...]
            acc_ref[HALO:] = jnp.zeros((PLANES, 2 * COILS, rows, GZ), jnp.float32)
        else:
            acc_ref[...] = jnp.zeros((PLANES + HALO, 2 * COILS, rows, GZ), jnp.float32)

    y_tab = y_ref[...]

    def step(index, _):
        for part in range(STEP):
            packed = gather(samples_ref, (index * STEP + part) * (LANES // CAP), q)
            build(packed, y_tab, pair_ref, dense_ref, part * LANES, LANES)
        product = lax.dot_general(
            pair_ref[...], dense_ref[...], (((1,), (1,)), ((), ())), preferred_element_type=jnp.float32
        )
        here = pl.ds(4 * q, SPAN)
        acc_ref[here] = acc_ref[here] + product.reshape(SPAN, 2 * COILS, rows, GZ)
        return 0

    lax.fori_loop(0, SOURCES * CAP // (STEP * LANES), step, 0)

    @pl.when(q == QS - 1)
    def _():
        z_tab = z_ref[...]
        lines = transform_z(acc_ref[0:PLANES], z_tab)
        if last:
            edge = transform_z(acc_ref[PLANES:], z_tab)
        for row in range(rows):
            half, owner, e = row // 16, row % 16 // 2, row % 2
            here = slice((2 * half + e) * GZ, (2 * half + e + 1) * GZ)
            for coil in range(COILS):
                line = lines[coil * rows + row]
                out_ref[owner * 2 + coil // 2, coil % 2, :, here] = jnp.concatenate(
                    [line[:, :GZ], line[:, GZ:]], 0
                ).astype(jnp.bfloat16)
            for coil in range(0, COILS, 2) if last else ():
                pieces = []
                for inner in range(2):
                    line = edge[(coil + inner) * rows + row]
                    pieces += [line[:, :GZ], line[:, GZ:]]
                out_ref[owner * 2 + coil // 2, 2, :, here] = jnp.concatenate(pieces, 0).astype(
                    jnp.bfloat16
                )
        if not last:
            carried_ref[...] = acc_ref[PLANES:]


def grid_chunk(samples, y_tab, z_tab, carry=None, part=0):
    last = carry is not None
    rows = y_tab.shape[0] // 2
    tiles, lanes = (3, rows // 8 * GZ) if last else (2, rows // 8 * GZ)
    size = SPAN * 2 * COILS * rows
    flops = 2 * size * GZ * SOURCES * CAP * QS + 2 * PLANES * COILS * rows * 4 * GZ * GZ
    in_specs = [
        pl.BlockSpec((SOURCES, 16, 2 * CAP), lambda q: (0, 0, 0)),
        pl.BlockSpec((2 * rows, GY), lambda q: (0, 0)),
        pl.BlockSpec((2 * GZ, 2 * GZ), lambda q: (0, 0)),
    ]
    out_specs = [pl.BlockSpec((GROUPS, tiles, 16, lanes), lambda q: (0, 0, 0, 0))]
    out_shape = [jax.ShapeDtypeStruct((GROUPS, tiles, 16, lanes), jnp.bfloat16)]
    operands = [samples, y_tab, z_tab]
    if last:
        in_specs.append(pl.BlockSpec((HALO, 2 * COILS, rows, GZ), lambda q: (0, 0, part, 0)))
        operands.append(carry)
    else:
        out_specs.append(pl.BlockSpec((HALO, 2 * COILS, rows, GZ), lambda q: (0, 0, 0, 0)))
        out_shape.append(jax.ShapeDtypeStruct((HALO, 2 * COILS, rows, GZ), jnp.float32))
    return pl.pallas_call(
        lambda *refs: grid_kernel(last, *refs),
        grid=(QS,),
        in_specs=in_specs,
        out_specs=out_specs,
        out_shape=out_shape,
        scratch_shapes=[
            pltpu.VMEM((size, STEP * LANES), jnp.bfloat16),
            pltpu.VMEM((GZ, STEP * LANES), jnp.bfloat16),
            pltpu.VMEM((PLANES + HALO, 2 * COILS, rows, GZ), jnp.float32),
        ],
        compiler_params=pltpu.CompilerParams(vmem_limit_bytes=48 * 2**20),
        cost_estimate=pl.CostEstimate(
            flops=2 * flops, bytes_accessed=4 * 2**20, transcendentals=0
        ),
        name="grid_chunk",
    )(*operands)


def combine_kernel(first_ref, second_ref, main_ref, edge_ref, maps_ref, out_ref):
    total = [None, None]
    depth = GROUPS * 16
    edge_rows = second_ref[:, 2].reshape(depth, GZ)
    for coil in range(2):
        image = jnp.dot(edge_ref[coil], edge_rows, preferred_element_type=jnp.float32)
        for chunk, ref in enumerate((first_ref, second_ref)):
            rows = ref[:, coil].reshape(depth, GZ)
            image = image + jnp.dot(main_ref[chunk], rows, preferred_element_type=jnp.float32)
        image_re, image_im = image[:GX], image[GX:]
        map_re = maps_ref[coil, 0].astype(jnp.float32)
        map_im = maps_ref[coil, 1].astype(jnp.float32)
        real = map_re * image_re + map_im * image_im
        imag = map_re * image_im - map_im * image_re
        total = [real, imag] if coil == 0 else [total[0] + real, total[1] + imag]
    for part in range(2):
        out_ref[:, part] = total[part].astype(jnp.bfloat16).reshape(8, GX // 8, GZ)


def combine(first, second, maps, half):
    main_tab, edge_tab = x_tables()
    depth = GROUPS * 16
    return pl.pallas_call(
        combine_kernel,
        grid=(2,),
        in_specs=[
            pl.BlockSpec((GROUPS, 2, 16, GZ), lambda y: (0, 0, 0, y + 2 * half)),
            pl.BlockSpec((GROUPS, 3, 16, GZ), lambda y: (0, 0, 0, y)),
            pl.BlockSpec((CHUNKS, 2 * GX, depth), lambda y: (0, 0, 0)),
            pl.BlockSpec((2, 2 * GX, depth), lambda y: (0, 0, 0)),
            pl.BlockSpec((2, 2, GX, GZ), lambda y: (0, 0, 0, y + 2 * half)),
        ],
        out_specs=pl.BlockSpec((8, 2, GX // 8, GZ), lambda y: (0, 0, 0, y)),
        out_shape=jax.ShapeDtypeStruct((8, 2, GX // 8, 2 * GZ), jnp.bfloat16),
        compiler_params=pltpu.CompilerParams(vmem_limit_bytes=48 * 2**20),
        cost_estimate=pl.CostEstimate(
            flops=2 * 2 * 2 * GX * 3 * depth * 2 * GZ, bytes_accessed=4 * 2**20, transcendentals=0
        ),
        name="combine",
    )(first, second, jnp.asarray(main_tab), jnp.asarray(edge_tab), maps)


def pack(values, offsets, cells, slots):
    used = slots < SLOTS
    kept = jnp.where(used[None, :], values.reshape(4, SLOTS), jnp.zeros((), jnp.bfloat16))
    spots = jnp.stack([cells // (GY * GZ), cells // GZ % GY, cells % GZ], 0).astype(jnp.bfloat16)
    about = jnp.where(lax.axis_index("core") == 0, offsets, spots)
    rows = jnp.concatenate([kept, about, jnp.zeros((1, SLOTS), jnp.bfloat16)], 0)
    return rows.reshape(8, GROUPS, CHUNKS, QS * CAP).transpose(2, 1, 0, 3)


def turn(array, axes):
    return lax.all_to_all(array, axes, split_axis=0, concat_axis=0, tiled=True)


def body(sample_values, sample_offsets, sample_cells, sample_slots, sensitivity):
    packed = pack(sample_values, sample_offsets, sample_cells, sample_slots)
    planes = ("zl", "x", "core")
    samples = []
    for chunk in range(CHUNKS):
        copies = jnp.broadcast_to(packed[chunk][None], (ZH,) + packed.shape[1:])
        got = turn(copies.reshape(ZH * GROUPS, 8, QS * CAP), ("zh",) + planes)
        samples.append(got.reshape(SOURCES, 16, QS * CAP))
    here = lax.axis_index("zh")

    def rows(part):
        return lax.dynamic_index_in_dim(jnp.asarray(y_table(part)), here, 0, keepdims=False)

    z_tab = jnp.asarray(z_table())
    first, carry = grid_chunk(samples[0], rows(None), z_tab)
    first = turn(first, planes)
    maps = sensitivity.reshape(2, 2, GX, 4 * GZ)
    images = []
    for half in range(2):
        (second,) = grid_chunk(samples[1], rows(half), z_tab, carry, half)
        partial = combine(first, turn(second, planes), maps, half)
        images.append(jnp.sum(turn(partial, ("y", "core")).astype(jnp.float32), axis=0))
    return jnp.concatenate(images, 2).reshape(2, GX // 8, 4, GZ)


def solution(mesh):
    fine = Mesh(mesh.devices.reshape(8, 2, 4, 4, 2), ("zh", "zl", "x", "y", "core"))
    space, coil = ("zh", "zl", "x"), ("y", "core")
    placed = (
        P(coil, None, space),
        P(None, space),
        P(space),
        P(space),
        P(coil, None, None, space, None),
    )
    return jax.shard_map(
        body, mesh=fine, in_specs=placed, out_specs=P(None, coil, space, None), check_vma=False
    )
```

```python
import math

import jax
import jax.numpy as jnp
import ml_dtypes
import numpy as np
from jax import lax
from jax.experimental import pallas as pl
from jax.experimental.pallas import tpu as pltpu
from jax.sharding import Mesh
from jax.sharding import PartitionSpec as P

GX = 256
GY = 256
GZ = 256
SLOTS = 4096
CAP = 64

BETA = 9.0
TERMS = 31

ZH = 8
SOURCES = 64
UNIT = 16
GROUPS = 16
BLOCKS = 4
CHUNKS = 2
LANES = 512
STEP = 2
COILS = 4
ROWS = 32
TAPS = 4
SPAN = 7
PAIR = 2 * COILS * ROWS
HALF = PAIR // 2
PLANES = 8
HALO = 4


def series():
    quarter = 0.25 * BETA * BETA
    terms = [quarter**k / float(math.factorial(k)) ** 2 for k in range(TERMS)]
    total = math.fsum(terms)
    return [float(np.float32(t / total)) for t in terms]


def waves():
    counter = np.arange(256)
    phase = (counter[:, None] * counter[None, :] % 256).astype(np.float32) * np.float32(
        2.0 * math.pi / 256
    )
    scale = np.float32(1.0 / 16.0)
    both = np.stack([np.cos(phase) * scale, np.sin(phase) * scale], 0)
    return both.astype(ml_dtypes.bfloat16).astype(np.float32)


def z_table():
    cosine, sine = waves()
    return np.block([[cosine, sine], [-sine, cosine]]).astype(ml_dtypes.bfloat16)


def y_table():
    both = waves().reshape(2, ZH, ROWS, 256)
    return both.transpose(1, 0, 2, 3).reshape(ZH, 2 * ROWS, 256).astype(ml_dtypes.bfloat16)


def x_columns(planes, part):
    cosine, sine = waves()
    if part == 0:
        return np.concatenate([cosine[:, planes], sine[:, planes]], 0)
    return np.concatenate([-sine[:, planes], cosine[:, planes]], 0)


def x_tables():
    main = []
    for chunk in range(CHUNKS):
        cols = []
        for group in range(GROUPS):
            planes = (16 * group + PLANES * chunk + np.arange(PLANES) - 1) % GX
            cols += [x_columns(planes, 0), x_columns(planes, 1)]
        main.append(np.concatenate(cols, 1))
    halo = []
    for coil in range(2):
        cols = []
        for group in range(GROUPS):
            planes = (16 * group + 16 + np.arange(HALO) - 1) % GX
            real = np.arange(HALO) < 3
            for other in range(2):
                keep = real & (other == coil)
                cols += [x_columns(planes, part) * keep for part in range(2)]
        halo.append(np.concatenate(cols, 1))
    return np.stack(main).astype(ml_dtypes.bfloat16), np.stack(halo).astype(ml_dtypes.bfloat16)


def tap_rows(first, second, lanes):
    row = lax.broadcasted_iota(jnp.int32, (8, lanes), 0)
    offset = jnp.where(row < TAPS, first, second)
    distance = offset + (1.0 - (row % TAPS).astype(jnp.float32))
    inner = jnp.maximum(1.0 - 0.25 * distance * distance, 0.0)
    coefficients = series()
    total = jnp.full((8, lanes), coefficients[-1], jnp.float32)
    for value in coefficients[-2::-1]:
        total = total * inner + value
    return total


def dense_rows(weights, base, lanes):
    high = base // 16
    low = base % 16
    row = lax.broadcasted_iota(jnp.int32, (16, lanes), 0)
    pattern = jnp.zeros((16, lanes), jnp.float32)
    for tap in range(TAPS):
        pattern = jnp.where(row == (low + tap) % 16, weights[tap], pattern)
    place = jnp.where(row < low, (high + 1) % 16, high).astype(jnp.float32)
    pattern = pattern.astype(jnp.bfloat16)
    place = place.astype(jnp.bfloat16)
    zero = jnp.zeros((16, lanes), jnp.bfloat16)
    return [
        jnp.where(place == jnp.bfloat16(block), pattern, zero) for block in range(16)
    ]


def build(packed, y_tab, pair_ref, dense_ref, at, lanes):
    taps_xy = tap_rows(packed[4:5], packed[5:6], lanes)
    taps_z = tap_rows(packed[6:7], packed[6:7], lanes)
    cell = packed.astype(jnp.int32)
    base_x = cell[12:13]
    base_y = (cell[13:14] + 255) % 256
    base_z = (cell[14:15] + 255) % 256
    z_blocks = dense_rows([taps_z[t : t + 1] for t in range(TAPS)], base_z, lanes)
    for block in range(16):
        dense_ref[block * 16 : (block + 1) * 16, at : at + lanes] = z_blocks[block]
    y_blocks = dense_rows([taps_xy[4 + t : 5 + t] for t in range(TAPS)], base_y, lanes)
    turn = jnp.dot(y_tab, jnp.concatenate(y_blocks, 0), preferred_element_type=jnp.float32)
    turn_re, turn_im = turn[:ROWS], turn[ROWS:]
    real, imag = [], []
    for coil in range(COILS):
        row = (coil // 2) * 8 + (coil % 2) * 2
        value_re, value_im = packed[row : row + 1], packed[row + 1 : row + 2]
        real.append((value_re * turn_re - value_im * turn_im).astype(jnp.bfloat16))
        imag.append((value_re * turn_im + value_im * turn_re).astype(jnp.bfloat16))
    values = real + imag
    row = lax.broadcasted_iota(jnp.int32, (8, lanes), 0)
    dense_x = jnp.zeros((8, lanes), jnp.float32)
    for tap in range(TAPS):
        dense_x = jnp.where(row == base_x + tap, taps_xy[tap : tap + 1], dense_x)
    for plane in range(SPAN):
        weight = jnp.broadcast_to(dense_x[plane : plane + 1], (ROWS, lanes)).astype(jnp.bfloat16)
        for part in range(2 * COILS):
            start = plane * PAIR + part * ROWS
            pair_ref[start : start + ROWS, at : at + lanes] = values[part] * weight


def transform_z(grid_planes, z_tab):
    planes = grid_planes.shape[0]
    grid = grid_planes.astype(jnp.bfloat16)
    joined = jnp.concatenate([grid[:, :HALF], grid[:, HALF:]], axis=2)
    along = jnp.dot(
        joined.reshape(planes * HALF, 2 * GZ), z_tab, preferred_element_type=jnp.float32
    )
    return jnp.swapaxes(along.reshape(planes, HALF, 2 * GZ), 0, 1)


def gather(samples_ref, start, offset):
    per = 128 // UNIT
    lane = lax.broadcasted_iota(jnp.int32, (16, 128), 1) // UNIT
    pieces = []
    for piece in range(LANES // 128):
        joined = None
        for k in range(per):
            rows = samples_ref[start + piece * per + k].astype(jnp.float32)
            rows = pltpu.roll(rows, (128 + UNIT * k - offset) % 128, 1)
            joined = rows if joined is None else jnp.where(lane == k, rows, joined)
        pieces.append(joined)
    return jnp.concatenate(pieces, 1)


def largest(samples_ref):
    def step(index, seen):
        return jnp.maximum(seen, jnp.abs(samples_ref[index].astype(jnp.float32)))

    seen = lax.fori_loop(0, SOURCES, step, jnp.zeros((16, 128), jnp.float32), unroll=8)
    row = lax.broadcasted_iota(jnp.int32, (16, 128), 0)
    return jnp.max(jnp.where(row % 8 < 4, seen, 0.0), axis=0, keepdims=True)


def grid_kernel(last, samples_ref, y_ref, z_ref, carry_ref, out_ref, carried_ref, pair_ref, dense_ref, acc_ref):
    q = pl.program_id(0)

    @pl.when(q == 0)
    def _():
        acc_ref[0:HALO] = carry_ref[...]
        acc_ref[HALO:] = jnp.zeros((PLANES, PAIR, GZ), jnp.float32)

    y_tab = y_ref[...]
    seen = largest(samples_ref)
    unit = lax.broadcasted_iota(jnp.int32, (1, 128), 1) // UNIT

    def step(index, _):
        place = q * (CAP // UNIT) + index

        @pl.when(jnp.max(jnp.where(unit == place, seen, 0.0)) > 0.0)
        def _():
            for part in range(STEP):
                packed = gather(samples_ref, part * (LANES // UNIT), place * UNIT)
                build(packed, y_tab, pair_ref, dense_ref, part * LANES, LANES)
            product = lax.dot_general(
                pair_ref[...],
                dense_ref[...],
                (((1,), (1,)), ((), ())),
                preferred_element_type=jnp.float32,
            )
            here = pl.ds(4 * q, SPAN)
            acc_ref[here] = acc_ref[here] + product.reshape(SPAN, PAIR, GZ)

        return 0

    lax.fori_loop(0, CAP // UNIT, step, 0)

    @pl.when(q == BLOCKS // CHUNKS - 1)
    def _():
        z_tab = z_ref[...]
        lines = transform_z(acc_ref[0:PLANES], z_tab)
        for coil in range(COILS):
            for row in range(ROWS):
                line = lines[coil * ROWS + row]
                both = jnp.concatenate([line[:, :GZ], line[:, GZ:]], 0).astype(jnp.bfloat16)
                out_ref[
                    (row // 4) * 2 + coil // 2, coil % 2, :, (row % 4) * GZ : (row % 4 + 1) * GZ
                ] = both
        if last:
            edge = transform_z(acc_ref[PLANES:], z_tab)
            for coil in range(0, COILS, 2):
                for row in range(ROWS):
                    pieces = []
                    for inner in range(2):
                        line = edge[(coil + inner) * ROWS + row]
                        pieces += [line[:, :GZ], line[:, GZ:]]
                    out_ref[
                        (row // 4) * 2 + coil // 2, 2, :, (row % 4) * GZ : (row % 4 + 1) * GZ
                    ] = jnp.concatenate(pieces, 0).astype(jnp.bfloat16)
        else:
            carried_ref[...] = acc_ref[PLANES:]


def grid_chunk(samples, y_tab, z_tab, carry, chunk):
    blocks = BLOCKS // CHUNKS
    last = chunk == CHUNKS - 1
    tiles = 3 if last else 2
    flops = 2 * SPAN * PAIR * GZ * SOURCES * CAP * blocks + 2 * PLANES * PAIR * GZ * 2 * GZ
    return pl.pallas_call(
        lambda *refs: grid_kernel(last, *refs),
        grid=(blocks,),
        in_specs=[
            pl.BlockSpec((SOURCES, 16, blocks * CAP), lambda q: (0, 0, chunk)),
            pl.BlockSpec((2 * ROWS, GY), lambda q: (0, 0)),
            pl.BlockSpec((2 * GZ, 2 * GZ), lambda q: (0, 0)),
            pl.BlockSpec((HALO, PAIR, GZ), lambda q: (0, 0, 0)),
        ],
        out_specs=[
            pl.BlockSpec((GROUPS, tiles, 16, 4 * GZ), lambda q: (0, 0, 0, 0)),
            pl.BlockSpec((HALO, PAIR, GZ), lambda q: (0, 0, 0)),
        ],
        out_shape=[
            jax.ShapeDtypeStruct((GROUPS, tiles, 16, 4 * GZ), jnp.bfloat16),
            jax.ShapeDtypeStruct((HALO, PAIR, GZ), jnp.float32),
        ],
        scratch_shapes=[
            pltpu.VMEM((SPAN * PAIR, STEP * LANES), jnp.bfloat16),
            pltpu.VMEM((GZ, STEP * LANES), jnp.bfloat16),
            pltpu.VMEM((PLANES + HALO, PAIR, GZ), jnp.float32),
        ],
        compiler_params=pltpu.CompilerParams(vmem_limit_bytes=48 * 2**20),
        cost_estimate=pl.CostEstimate(
            flops=flops, bytes_accessed=4 * 2**20, transcendentals=0
        ),
        name="grid_chunk",
    )(samples, y_tab, z_tab, carry)


def combine_kernel(first_ref, second_ref, main_ref, edge_ref, maps_ref, out_ref):
    total = [None, None]
    depth = GROUPS * 16
    edge_rows = second_ref[:, 2].reshape(depth, GZ)
    for coil in range(2):
        image = jnp.dot(edge_ref[coil], edge_rows, preferred_element_type=jnp.float32)
        for chunk, ref in enumerate((first_ref, second_ref)):
            rows = ref[:, coil].reshape(depth, GZ)
            image = image + jnp.dot(main_ref[chunk], rows, preferred_element_type=jnp.float32)
        image_re, image_im = image[:GX], image[GX:]
        map_re = maps_ref[coil, 0].astype(jnp.float32)
        map_im = maps_ref[coil, 1].astype(jnp.float32)
        real = map_re * image_re + map_im * image_im
        imag = map_re * image_im - map_im * image_re
        total = [real, imag] if coil == 0 else [total[0] + real, total[1] + imag]
    for part in range(2):
        out_ref[:, part] = total[part].astype(jnp.bfloat16).reshape(8, GX // 8, GZ)


def combine(first, second, maps):
    main_tab, edge_tab = x_tables()
    depth = GROUPS * 16
    return pl.pallas_call(
        combine_kernel,
        grid=(4,),
        in_specs=[
            pl.BlockSpec((GROUPS, 2, 16, GZ), lambda y: (0, 0, 0, y)),
            pl.BlockSpec((GROUPS, 3, 16, GZ), lambda y: (0, 0, 0, y)),
            pl.BlockSpec((CHUNKS, 2 * GX, depth), lambda y: (0, 0, 0)),
            pl.BlockSpec((2, 2 * GX, depth), lambda y: (0, 0, 0)),
            pl.BlockSpec((2, 2, GX, GZ), lambda y: (0, 0, 0, y)),
        ],
        out_specs=pl.BlockSpec((8, 2, GX // 8, GZ), lambda y: (0, 0, 0, y)),
        out_shape=jax.ShapeDtypeStruct((8, 2, GX // 8, 4 * GZ), jnp.bfloat16),
        compiler_params=pltpu.CompilerParams(vmem_limit_bytes=48 * 2**20),
        cost_estimate=pl.CostEstimate(
            flops=2 * 2 * 2 * GX * 3 * depth * 4 * GZ, bytes_accessed=8 * 2**20, transcendentals=0
        ),
        name="combine",
    )(first, second, jnp.asarray(main_tab), jnp.asarray(edge_tab), maps)


def pack_kernel(values_ref, offsets_ref, cells_ref, slots_ref, out_ref):
    used = slots_ref[...] < SLOTS
    cells = cells_ref[...]
    rows = [jnp.where(used, values_ref[r : r + 1].astype(jnp.float32), 0.0) for r in range(4)]
    spots = (cells // (GY * GZ), cells // GZ % GY, cells % GZ)
    first = lax.axis_index("core") == 0
    for axis in range(3):
        offset = offsets_ref[axis : axis + 1].astype(jnp.float32)
        rows.append(jnp.where(first, offset, spots[axis].astype(jnp.float32)))
    rows.append(jnp.zeros((1, SLOTS), jnp.float32))
    packed = jnp.concatenate(rows, 0).astype(jnp.bfloat16)
    width = BLOCKS * CAP
    for group in range(GROUPS):
        part = packed[:, group * width : (group + 1) * width]
        for copy in range(ZH):
            out_ref[copy * GROUPS + group] = part


def pack(values, offsets, cells, slots):
    return pl.pallas_call(
        pack_kernel,
        out_shape=jax.ShapeDtypeStruct((ZH * GROUPS, 8, BLOCKS * CAP), jnp.bfloat16),
        compiler_params=pltpu.CompilerParams(vmem_limit_bytes=16 * 2**20),
        name="pack",
    )(values.reshape(4, SLOTS), offsets, cells.reshape(1, SLOTS), slots.reshape(1, SLOTS))


def turn(array, axes):
    return lax.all_to_all(array, axes, split_axis=0, concat_axis=0, tiled=True)


def body(sample_values, sample_offsets, sample_cells, sample_slots, sensitivity):
    packed = pack(sample_values, sample_offsets, sample_cells, sample_slots)
    planes = ("zl", "x", "core")
    got = turn(packed, ("zh",) + planes)
    samples = got.reshape(SOURCES, 16, BLOCKS * CAP)
    y_tab = lax.dynamic_index_in_dim(
        jnp.asarray(y_table()), lax.axis_index("zh"), 0, keepdims=False
    )
    z_tab = jnp.asarray(z_table())
    carry = jnp.zeros((HALO, PAIR, GZ), jnp.float32)
    turned = []
    for chunk in range(CHUNKS):
        part, carry = grid_chunk(samples, y_tab, z_tab, carry, chunk)
        turned.append(turn(part, planes))
    maps = sensitivity.reshape(2, 2, GX, 4 * GZ)
    partial = turn(combine(*turned, maps), ("y", "core"))
    image = jnp.sum(partial.astype(jnp.float32), axis=0)
    return image.reshape(2, GX // 8, 4, GZ)


def solution(mesh):
    fine = Mesh(mesh.devices.reshape(8, 2, 4, 4, 2), ("zh", "zl", "x", "y", "core"))
    space, coil = ("zh", "zl", "x"), ("y", "core")
    placed = (
        P(coil, None, space),
        P(None, space),
        P(space),
        P(space),
        P(coil, None, None, space, None),
    )
    return jax.shard_map(
        body, mesh=fine, in_specs=placed, out_specs=P(None, coil, space, None), check_vma=False
    )
```

```python
import math

import jax
import jax.numpy as jnp
import ml_dtypes
import numpy as np
from jax import lax
from jax.experimental import pallas as pl
from jax.experimental.pallas import tpu as pltpu
from jax.sharding import Mesh
from jax.sharding import PartitionSpec as P

GX = 256
GY = 256
GZ = 256
SLOTS = 4096
CAP = 64

BETA = 9.0
TERMS = 31

ZH = 8
SOURCES = 64
UNIT = 16
GROUPS = 16
BLOCKS = 4
LANES = 256
STEP = 4
COILS = 4
ROWS = 32
TAPS = 4
SPAN = 7
PAIR = 2 * COILS * ROWS
HALF = PAIR // 2
PLANES = 16
HALO = 4


def series():
    quarter = 0.25 * BETA * BETA
    terms = [quarter**k / float(math.factorial(k)) ** 2 for k in range(TERMS)]
    total = math.fsum(terms)
    return [float(np.float32(t / total)) for t in terms]


def waves():
    counter = np.arange(256)
    phase = (counter[:, None] * counter[None, :] % 256).astype(np.float32) * np.float32(
        2.0 * math.pi / 256
    )
    scale = np.float32(1.0 / 16.0)
    both = np.stack([np.cos(phase) * scale, np.sin(phase) * scale], 0)
    return both.astype(ml_dtypes.bfloat16).astype(np.float32)


def z_table():
    cosine, sine = waves()
    return np.block([[cosine, sine], [-sine, cosine]]).astype(ml_dtypes.bfloat16)


def y_table():
    both = waves().reshape(2, ZH, ROWS, 256)
    return both.transpose(1, 0, 2, 3).reshape(ZH, 2 * ROWS, 256).astype(ml_dtypes.bfloat16)


def x_columns(planes, part):
    cosine, sine = waves()
    if part == 0:
        return np.concatenate([cosine[:, planes], sine[:, planes]], 0)
    return np.concatenate([-sine[:, planes], cosine[:, planes]], 0)


def x_tables():
    main = []
    for group in range(GROUPS):
        for half in range(2):
            planes = (PLANES * group + 8 * half + np.arange(8) - 1) % GX
            main += [x_columns(planes, 0), x_columns(planes, 1)]
    halo = []
    for coil in range(2):
        cols = []
        for group in range(GROUPS):
            planes = (PLANES * group + PLANES + np.arange(HALO) - 1) % GX
            real = np.arange(HALO) < 3
            for other in range(2):
                keep = real & (other == coil)
                cols += [x_columns(planes, part) * keep for part in range(2)]
        halo.append(np.concatenate(cols, 1))
    return np.concatenate(main, 1).astype(ml_dtypes.bfloat16), np.stack(halo).astype(ml_dtypes.bfloat16)


def tap_rows(first, second, lanes):
    row = lax.broadcasted_iota(jnp.int32, (8, lanes), 0)
    offset = jnp.where(row < TAPS, first, second)
    distance = offset + (1.0 - (row % TAPS).astype(jnp.float32))
    inner = jnp.maximum(1.0 - 0.25 * distance * distance, 0.0)
    coefficients = series()
    total = jnp.full((8, lanes), coefficients[-1], jnp.float32)
    for value in coefficients[-2::-1]:
        total = total * inner + value
    return total


def dense_rows(weights, base, lanes):
    high = base // 16
    low = base % 16
    row = lax.broadcasted_iota(jnp.int32, (16, lanes), 0)
    pattern = jnp.zeros((16, lanes), jnp.float32)
    for tap in range(TAPS):
        pattern = jnp.where(row == (low + tap) % 16, weights[tap], pattern)
    place = jnp.where(row < low, (high + 1) % 16, high).astype(jnp.float32)
    pattern = pattern.astype(jnp.bfloat16)
    place = place.astype(jnp.bfloat16)
    zero = jnp.zeros((16, lanes), jnp.bfloat16)
    return [
        jnp.where(place == jnp.bfloat16(block), pattern, zero) for block in range(16)
    ]


def build(packed, y_tab, pair_ref, dense_ref, at, lanes):
    taps_xy = tap_rows(packed[4:5], packed[5:6], lanes)
    taps_z = tap_rows(packed[6:7], packed[6:7], lanes)
    cell = packed.astype(jnp.int32)
    base_x = cell[12:13]
    base_y = (cell[13:14] + 255) % 256
    base_z = (cell[14:15] + 255) % 256
    z_blocks = dense_rows([taps_z[t : t + 1] for t in range(TAPS)], base_z, lanes)
    for block in range(16):
        dense_ref[block * 16 : (block + 1) * 16, at : at + lanes] = z_blocks[block]
    y_blocks = dense_rows([taps_xy[4 + t : 5 + t] for t in range(TAPS)], base_y, lanes)
    turn = jnp.dot(y_tab, jnp.concatenate(y_blocks, 0), preferred_element_type=jnp.float32)
    turn_re, turn_im = turn[:ROWS], turn[ROWS:]
    real, imag = [], []
    for coil in range(COILS):
        row = (coil // 2) * 8 + (coil % 2) * 2
        value_re, value_im = packed[row : row + 1], packed[row + 1 : row + 2]
        real.append((value_re * turn_re - value_im * turn_im).astype(jnp.bfloat16))
        imag.append((value_re * turn_im + value_im * turn_re).astype(jnp.bfloat16))
    values = real + imag
    row = lax.broadcasted_iota(jnp.int32, (8, lanes), 0)
    dense_x = jnp.zeros((8, lanes), jnp.float32)
    for tap in range(TAPS):
        dense_x = jnp.where(row == base_x + tap, taps_xy[tap : tap + 1], dense_x)
    for plane in range(SPAN):
        weight = jnp.broadcast_to(dense_x[plane : plane + 1], (ROWS, lanes)).astype(jnp.bfloat16)
        for part in range(2 * COILS):
            start = plane * PAIR + part * ROWS
            pair_ref[start : start + ROWS, at : at + lanes] = values[part] * weight


def transform_z(grid_planes, z_tab):
    planes = grid_planes.shape[0]
    grid = grid_planes.astype(jnp.bfloat16)
    joined = jnp.concatenate([grid[:, :HALF], grid[:, HALF:]], axis=2)
    along = jnp.dot(
        joined.reshape(planes * HALF, 2 * GZ), z_tab, preferred_element_type=jnp.float32
    )
    return jnp.swapaxes(along.reshape(planes, HALF, 2 * GZ), 0, 1)


def gather(samples_ref, start, half, offset):
    per = 128 // UNIT
    lane = lax.broadcasted_iota(jnp.int32, (16, 128), 1) // UNIT
    pieces = []
    for piece in range(LANES // 128):
        joined = None
        for k in range(per):
            rows = samples_ref[half, start + piece * per + k].astype(jnp.float32)
            rows = pltpu.roll(rows, (128 + UNIT * k - offset) % 128, 1)
            joined = rows if joined is None else jnp.where(lane == k, rows, joined)
        pieces.append(joined)
    return jnp.concatenate(pieces, 1)


def largest(samples_ref, half):
    def step(index, seen):
        return jnp.maximum(seen, jnp.abs(samples_ref[half, index].astype(jnp.float32)))

    seen = lax.fori_loop(0, SOURCES, step, jnp.zeros((16, 128), jnp.float32), unroll=8)
    row = lax.broadcasted_iota(jnp.int32, (16, 128), 0)
    return jnp.max(jnp.where(row % 8 < 4, seen, 0.0), axis=0, keepdims=True)


def grid_kernel(source_ref, y_ref, z_ref, out_ref, samples_ref, pair_ref, dense_ref, acc_ref, list_ref):
    for half in range(2):
        samples_ref[half] = source_ref[:, :, half * 128 : (half + 1) * 128]
    units = 128 // UNIT
    unit = lax.broadcasted_iota(jnp.int32, (1, 128), 1) // UNIT
    count = jnp.int32(0)
    for half in range(2):
        seen = largest(samples_ref, half)
        for place in range(units):
            list_ref[count] = half * units + place
            some = jnp.max(jnp.where(unit == place, seen, 0.0)) > 0.0
            count = count + some.astype(jnp.int32)
    acc_ref[...] = jnp.zeros(acc_ref.shape, jnp.float32)
    y_tab = y_ref[...]

    def step(index, _):
        block = list_ref[index]
        for part in range(STEP):
            start = part * (LANES // UNIT)
            packed = gather(samples_ref, start, block // units, block % units * UNIT)
            build(packed, y_tab, pair_ref, dense_ref, part * LANES, LANES)
        here = pl.ds(4 * (block // (CAP // UNIT)), SPAN)
        product = lax.dot_general(
            pair_ref[...], dense_ref[...], (((1,), (1,)), ((), ())), preferred_element_type=jnp.float32
        )
        acc_ref[here] = acc_ref[here] + product.reshape(SPAN, PAIR, GZ)
        return 0

    lax.fori_loop(0, count, step, 0)

    z_tab = z_ref[...]
    for first in range(0, PLANES, 8):
        lines = transform_z(acc_ref[first : first + 8], z_tab)
        for coil in range(COILS):
            for row in range(ROWS):
                line = lines[coil * ROWS + row]
                for part in range(2):
                    out_ref[
                        (row // 4) * 2 + coil // 2,
                        (coil % 2) * 2 + first // 8,
                        part * 8 : part * 8 + 8,
                        (row % 4) * GZ : (row % 4 + 1) * GZ,
                    ] = line[:, part * GZ : (part + 1) * GZ].astype(jnp.bfloat16)
    edge = transform_z(acc_ref[PLANES:], z_tab)
    for coil in range(0, COILS, 2):
        for row in range(ROWS):
            pieces = []
            for inner in range(2):
                line = edge[(coil + inner) * ROWS + row]
                pieces += [line[:, :GZ], line[:, GZ:]]
            out_ref[
                (row // 4) * 2 + coil // 2, 4, :, (row % 4) * GZ : (row % 4 + 1) * GZ
            ] = jnp.concatenate(pieces, 0).astype(jnp.bfloat16)


def grid_all(samples, y_tab, z_tab):
    flops = 2 * SPAN * PAIR * GZ * SOURCES * CAP * BLOCKS
    return pl.pallas_call(
        grid_kernel,
        out_shape=jax.ShapeDtypeStruct((GROUPS, 5, 16, 4 * GZ), jnp.bfloat16),
        scratch_shapes=[
            pltpu.VMEM((2, SOURCES, 16, 128), jnp.bfloat16),
            pltpu.VMEM((SPAN * PAIR, STEP * LANES), jnp.bfloat16),
            pltpu.VMEM((GZ, STEP * LANES), jnp.bfloat16),
            pltpu.VMEM((PLANES + HALO, PAIR, GZ), jnp.float32),
            pltpu.SMEM((17,), jnp.int32),
        ],
        compiler_params=pltpu.CompilerParams(vmem_limit_bytes=56 * 2**20),
        cost_estimate=pl.CostEstimate(
            flops=flops, bytes_accessed=4 * 2**20, transcendentals=0
        ),
        name="grid_all",
    )(samples, y_tab, z_tab)


def combine_kernel(turned_ref, main_ref, edge_ref, maps_ref, out_ref):
    total = [None, None]
    depth = GROUPS * 16
    edge_rows = turned_ref[:, 4].reshape(depth, GZ)
    for coil in range(2):
        rows = turned_ref[:, 2 * coil : 2 * coil + 2].reshape(2 * depth, GZ)
        image = jnp.dot(main_ref[...], rows, preferred_element_type=jnp.float32) + jnp.dot(
            edge_ref[coil], edge_rows, preferred_element_type=jnp.float32
        )
        image_re, image_im = image[:GX], image[GX:]
        map_re = maps_ref[coil, 0].astype(jnp.float32)
        map_im = maps_ref[coil, 1].astype(jnp.float32)
        real = map_re * image_re + map_im * image_im
        imag = map_re * image_im - map_im * image_re
        total = [real, imag] if coil == 0 else [total[0] + real, total[1] + imag]
    for part in range(2):
        out_ref[:, part] = total[part].astype(jnp.bfloat16).reshape(8, GX // 8, GZ)


def combine(turned, maps):
    main_tab, edge_tab = x_tables()
    depth = GROUPS * 16
    return pl.pallas_call(
        combine_kernel,
        grid=(4,),
        in_specs=[
            pl.BlockSpec((GROUPS, 5, 16, GZ), lambda y: (0, 0, 0, y)),
            pl.BlockSpec((2 * GX, 2 * depth), lambda y: (0, 0)),
            pl.BlockSpec((2, 2 * GX, depth), lambda y: (0, 0, 0)),
            pl.BlockSpec((2, 2, GX, GZ), lambda y: (0, 0, 0, y)),
        ],
        out_specs=pl.BlockSpec((8, 2, GX // 8, GZ), lambda y: (0, 0, 0, y)),
        out_shape=jax.ShapeDtypeStruct((8, 2, GX // 8, 4 * GZ), jnp.bfloat16),
        compiler_params=pltpu.CompilerParams(vmem_limit_bytes=56 * 2**20),
        cost_estimate=pl.CostEstimate(
            flops=2 * 2 * 2 * GX * 3 * depth * 4 * GZ, bytes_accessed=8 * 2**20, transcendentals=0
        ),
        name="combine",
    )(turned, jnp.asarray(main_tab), jnp.asarray(edge_tab), maps)


def pack_kernel(values_ref, offsets_ref, cells_ref, slots_ref, out_ref):
    used = slots_ref[...] < SLOTS
    cells = cells_ref[...]
    values = [values_ref[coil].astype(jnp.float32) for coil in range(2)]
    rows = [jnp.where(used, values[r // 2][r % 2 : r % 2 + 1], 0.0) for r in range(4)]
    spots = (cells // (GY * GZ), cells // GZ % GY, cells % GZ)
    first = lax.axis_index("core") == 0
    for axis in range(3):
        offset = offsets_ref[axis : axis + 1].astype(jnp.float32)
        rows.append(jnp.where(first, offset, spots[axis].astype(jnp.float32)))
    rows.append(jnp.zeros((1, SLOTS), jnp.float32))
    packed = jnp.concatenate(rows, 0).astype(jnp.bfloat16)
    width = BLOCKS * CAP
    for group in range(GROUPS):
        part = packed[:, group * width : (group + 1) * width]
        for copy in range(ZH):
            out_ref[copy * GROUPS + group] = part


def pack(values, offsets, cells, slots):
    return pl.pallas_call(
        pack_kernel,
        out_shape=jax.ShapeDtypeStruct((ZH * GROUPS, 8, BLOCKS * CAP), jnp.bfloat16),
        compiler_params=pltpu.CompilerParams(vmem_limit_bytes=56 * 2**20),
        name="pack",
    )(values, offsets, cells.reshape(1, SLOTS), slots.reshape(1, SLOTS))


def turn(array, axes):
    return lax.all_to_all(array, axes, split_axis=0, concat_axis=0, tiled=True)


def body(sample_values, sample_offsets, sample_cells, sample_slots, sensitivity):
    packed = pack(sample_values, sample_offsets, sample_cells, sample_slots)
    planes = ("zl", "x", "core")
    got = turn(packed, ("zh",) + planes)
    samples = got.reshape(SOURCES, 16, BLOCKS * CAP)
    y_tab = lax.dynamic_index_in_dim(
        jnp.asarray(y_table()), lax.axis_index("zh"), 0, keepdims=False
    )
    z_tab = jnp.asarray(z_table())
    turned = turn(grid_all(samples, y_tab, z_tab), planes)
    maps = sensitivity.reshape(2, 2, GX, 4 * GZ)
    partial = turn(combine(turned, maps), ("y", "core"))
    image = jnp.sum(partial.astype(jnp.float32), axis=0)
    return image.reshape(2, GX // 8, 4, GZ)


def solution(mesh):
    fine = Mesh(mesh.devices.reshape(8, 2, 4, 4, 2), ("zh", "zl", "x", "y", "core"))
    space, coil = ("zh", "zl", "x"), ("y", "core")
    placed = (
        P(coil, None, space),
        P(None, space),
        P(space),
        P(space),
        P(coil, None, None, space, None),
    )
    return jax.shard_map(
        body, mesh=fine, in_specs=placed, out_specs=P(None, coil, space, None), check_vma=False
    )
```

```python
import math

import jax
import jax.numpy as jnp
import ml_dtypes
import numpy as np
from jax import lax
from jax.experimental import pallas as pl
from jax.experimental.pallas import tpu as pltpu
from jax.sharding import Mesh
from jax.sharding import PartitionSpec as P

GX = 256
GY = 256
GZ = 256
SLOTS = 4096
CAP = 64

BETA = 9.0
TERMS = 31

ZH = 8
SOURCES = 64
UNIT = 16
GROUPS = 16
BLOCKS = 4
LANES = 256
STEP = 4
COILS = 4
ROWS = 32
TAPS = 4
SPAN = 7
PAIR = 2 * COILS * ROWS
HALF = PAIR // 2
CHUNKS = 2
PLANES = 8
HALO = 4


def series():
    quarter = 0.25 * BETA * BETA
    terms = [quarter**k / float(math.factorial(k)) ** 2 for k in range(TERMS)]
    total = math.fsum(terms)
    return [float(np.float32(t / total)) for t in terms]


def waves():
    counter = np.arange(256)
    phase = (counter[:, None] * counter[None, :] % 256).astype(np.float32) * np.float32(
        2.0 * math.pi / 256
    )
    scale = np.float32(1.0 / 16.0)
    both = np.stack([np.cos(phase) * scale, np.sin(phase) * scale], 0)
    return both.astype(ml_dtypes.bfloat16).astype(np.float32)


def z_table():
    cosine, sine = waves()
    return np.block([[cosine, sine], [-sine, cosine]]).astype(ml_dtypes.bfloat16)


def y_table():
    both = waves().reshape(2, ZH, ROWS, 256)
    return both.transpose(1, 0, 2, 3).reshape(ZH, 2 * ROWS, 256).astype(ml_dtypes.bfloat16)


def x_columns(planes, part):
    cosine, sine = waves()
    if part == 0:
        return np.concatenate([cosine[:, planes], sine[:, planes]], 0)
    return np.concatenate([-sine[:, planes], cosine[:, planes]], 0)


def x_tables():
    main = []
    for chunk in range(CHUNKS):
        cols = []
        for group in range(GROUPS):
            planes = (16 * group + PLANES * chunk + np.arange(PLANES) - 1) % GX
            cols += [x_columns(planes, 0), x_columns(planes, 1)]
        main.append(np.concatenate(cols, 1))
    halo = []
    for coil in range(2):
        cols = []
        for group in range(GROUPS):
            planes = (16 * group + 16 + np.arange(HALO) - 1) % GX
            real = np.arange(HALO) < 3
            for other in range(2):
                keep = real & (other == coil)
                cols += [x_columns(planes, part) * keep for part in range(2)]
        halo.append(np.concatenate(cols, 1))
    return np.stack(main).astype(ml_dtypes.bfloat16), np.stack(halo).astype(ml_dtypes.bfloat16)


def tap_rows(first, second, lanes):
    row = lax.broadcasted_iota(jnp.int32, (8, lanes), 0)
    offset = jnp.where(row < TAPS, first, second)
    distance = offset + (1.0 - (row % TAPS).astype(jnp.float32))
    inner = jnp.maximum(1.0 - 0.25 * distance * distance, 0.0)
    coefficients = series()
    total = jnp.full((8, lanes), coefficients[-1], jnp.float32)
    for value in coefficients[-2::-1]:
        total = total * inner + value
    return total


def dense_rows(weights, base, lanes):
    high = base // 16
    low = base % 16
    row = lax.broadcasted_iota(jnp.int32, (16, lanes), 0)
    pattern = jnp.zeros((16, lanes), jnp.float32)
    for tap in range(TAPS):
        pattern = jnp.where(row == (low + tap) % 16, weights[tap], pattern)
    place = jnp.where(row < low, (high + 1) % 16, high).astype(jnp.float32)
    pattern = pattern.astype(jnp.bfloat16)
    place = place.astype(jnp.bfloat16)
    zero = jnp.zeros((16, lanes), jnp.bfloat16)
    return [
        jnp.where(place == jnp.bfloat16(block), pattern, zero) for block in range(16)
    ]


def build(packed, y_tab, pair_ref, dense_ref, at, lanes):
    taps_xy = tap_rows(packed[4:5], packed[5:6], lanes)
    taps_z = tap_rows(packed[6:7], packed[6:7], lanes)
    cell = packed.astype(jnp.int32)
    base_x = cell[12:13]
    base_y = (cell[13:14] + 255) % 256
    base_z = (cell[14:15] + 255) % 256
    z_blocks = dense_rows([taps_z[t : t + 1] for t in range(TAPS)], base_z, lanes)
    for block in range(16):
        dense_ref[block * 16 : (block + 1) * 16, at : at + lanes] = z_blocks[block]
    y_blocks = dense_rows([taps_xy[4 + t : 5 + t] for t in range(TAPS)], base_y, lanes)
    turn = jnp.dot(y_tab, jnp.concatenate(y_blocks, 0), preferred_element_type=jnp.float32)
    turn_re, turn_im = turn[:ROWS], turn[ROWS:]
    real, imag = [], []
    for coil in range(COILS):
        row = (coil // 2) * 8 + (coil % 2) * 2
        value_re, value_im = packed[row : row + 1], packed[row + 1 : row + 2]
        real.append((value_re * turn_re - value_im * turn_im).astype(jnp.bfloat16))
        imag.append((value_re * turn_im + value_im * turn_re).astype(jnp.bfloat16))
    values = real + imag
    row = lax.broadcasted_iota(jnp.int32, (8, lanes), 0)
    dense_x = jnp.zeros((8, lanes), jnp.float32)
    for tap in range(TAPS):
        dense_x = jnp.where(row == base_x + tap, taps_xy[tap : tap + 1], dense_x)
    for plane in range(SPAN):
        weight = jnp.broadcast_to(dense_x[plane : plane + 1], (ROWS, lanes)).astype(jnp.bfloat16)
        for part in range(2 * COILS):
            start = plane * PAIR + part * ROWS
            pair_ref[start : start + ROWS, at : at + lanes] = values[part] * weight


def transform_z(grid_planes, z_tab):
    planes = grid_planes.shape[0]
    grid = grid_planes.astype(jnp.bfloat16)
    joined = jnp.concatenate([grid[:, :HALF], grid[:, HALF:]], axis=2)
    along = jnp.dot(
        joined.reshape(planes * HALF, 2 * GZ), z_tab, preferred_element_type=jnp.float32
    )
    return jnp.swapaxes(along.reshape(planes, HALF, 2 * GZ), 0, 1)


def gather(samples_ref, start, offset):
    per = 128 // UNIT
    lane = lax.broadcasted_iota(jnp.int32, (16, 128), 1) // UNIT
    pieces = []
    for piece in range(LANES // 128):
        joined = None
        for k in range(per):
            rows = samples_ref[start + piece * per + k].astype(jnp.float32)
            rows = pltpu.roll(rows, (128 + UNIT * k - offset) % 128, 1)
            joined = rows if joined is None else jnp.where(lane == k, rows, joined)
        pieces.append(joined)
    return jnp.concatenate(pieces, 1)


def filled(samples_ref):
    def step(index, seen):
        return jnp.maximum(seen, jnp.abs(samples_ref[index].astype(jnp.float32)))

    seen = lax.fori_loop(0, SOURCES, step, jnp.zeros((16, 128), jnp.float32), unroll=8)
    row = lax.broadcasted_iota(jnp.int32, (16, 128), 0)
    seen = jnp.max(jnp.where(row % 8 < 4, seen, 0.0), axis=0, keepdims=True)
    seen = jnp.broadcast_to(seen, (8, 128))
    for shift in (8, 4, 2, 1):
        seen = jnp.maximum(seen, pltpu.roll(seen, shift, 1))
    lane = lax.broadcasted_iota(jnp.int32, (8, 128), 1)
    place = lax.broadcasted_iota(jnp.int32, (8, 128), 0)
    hit = (seen > 0.0) & (lane == place * UNIT + UNIT - 1)
    return jnp.sum(jnp.where(hit, (1 << place).astype(jnp.float32), 0.0)).astype(jnp.int32)


def grid_kernel(last, samples_ref, y_ref, z_ref, *refs):
    if last:
        carry_ref, out_ref, pair_ref, dense_ref, acc_ref, list_ref = refs
    else:
        out_ref, carried_ref, pair_ref, dense_ref, acc_ref, list_ref = refs
    bits = filled(samples_ref)
    count = jnp.int32(0)
    for place in range(128 // UNIT):
        list_ref[count] = place
        count = count + ((bits >> place) & 1)
    if last:
        acc_ref[0:HALO] = carry_ref[...]
        acc_ref[HALO:] = jnp.zeros((PLANES, PAIR, GZ), jnp.float32)
    else:
        acc_ref[...] = jnp.zeros((PLANES + HALO, PAIR, GZ), jnp.float32)
    y_tab = y_ref[...]

    def step(index, _):
        block = list_ref[index]
        for part in range(STEP):
            packed = gather(samples_ref, part * (LANES // UNIT), block * UNIT)
            build(packed, y_tab, pair_ref, dense_ref, part * LANES, LANES)
        here = pl.ds(4 * (block // (CAP // UNIT)), SPAN)
        product = lax.dot_general(
            pair_ref[...], dense_ref[...], (((1,), (1,)), ((), ())), preferred_element_type=jnp.float32
        )
        acc_ref[here] = acc_ref[here] + product.reshape(SPAN, PAIR, GZ)
        return 0

    lax.fori_loop(0, count, step, 0)

    z_tab = z_ref[...]
    lines = transform_z(acc_ref[0:PLANES], z_tab)
    if last:
        edge = transform_z(acc_ref[PLANES:], z_tab)
    else:
        carried_ref[...] = acc_ref[PLANES:]
    for row in range(ROWS):
        owner = (row // 4) * 2 + row % 4 // 2
        here = slice(row % 2 * GZ, (row % 2 + 1) * GZ)
        for coil in range(COILS):
            line = lines[coil * ROWS + row]
            out_ref[owner, coil, :, here] = jnp.concatenate([line[:, :GZ], line[:, GZ:]], 0).astype(
                jnp.bfloat16
            )
        for pair in range(COILS // 2) if last else ():
            pieces = []
            for inner in range(2):
                line = edge[(2 * pair + inner) * ROWS + row]
                pieces += [line[:, :GZ], line[:, GZ:]]
            out_ref[owner, COILS + pair, :, here] = jnp.concatenate(pieces, 0).astype(jnp.bfloat16)


def grid_chunk(samples, y_tab, z_tab, chunk, carry=None):
    last = carry is not None
    tiles = COILS + (COILS // 2 if last else 0)
    flops = 2 * SPAN * PAIR * GZ * SOURCES * CAP * BLOCKS // CHUNKS
    edges = (HALO, PAIR, GZ)
    in_specs = [
        pl.BlockSpec((SOURCES, 16, 128), lambda q: (0, 0, chunk)),
        pl.BlockSpec((2 * ROWS, GY), lambda q: (0, 0)),
        pl.BlockSpec((2 * GZ, 2 * GZ), lambda q: (0, 0)),
    ]
    out_specs = [pl.BlockSpec((GROUPS, tiles, 16, 2 * GZ), lambda q: (0, 0, 0, 0))]
    out_shape = [jax.ShapeDtypeStruct((GROUPS, tiles, 16, 2 * GZ), jnp.bfloat16)]
    operands = [samples, y_tab, z_tab]
    if last:
        in_specs.append(pl.BlockSpec(edges, lambda q: (0, 0, 0)))
        operands.append(carry)
    else:
        out_specs.append(pl.BlockSpec(edges, lambda q: (0, 0, 0)))
        out_shape.append(jax.ShapeDtypeStruct(edges, jnp.float32))
    return pl.pallas_call(
        lambda *refs: grid_kernel(last, *refs),
        grid=(1,),
        in_specs=in_specs,
        out_specs=out_specs,
        out_shape=out_shape,
        scratch_shapes=[
            pltpu.VMEM((SPAN * PAIR, STEP * LANES), jnp.bfloat16),
            pltpu.VMEM((GZ, STEP * LANES), jnp.bfloat16),
            pltpu.VMEM((PLANES + HALO, PAIR, GZ), jnp.float32),
            pltpu.SMEM((9,), jnp.int32),
        ],
        compiler_params=pltpu.CompilerParams(vmem_limit_bytes=36 * 2**20),
        cost_estimate=pl.CostEstimate(flops=flops, bytes_accessed=4 * 2**20, transcendentals=0),
        name="grid_chunk",
    )(*operands)


def combine_kernel(first_ref, second_ref, main_ref, edge_ref, own_ref, other_ref, out_ref):
    core = lax.axis_index("core")
    total = [None, None]
    depth = GROUPS * 16
    for maps_ref, pair in ((own_ref, core), (other_ref, 1 - core)):
        edge_rows = second_ref[:, COILS + pair].reshape(depth, GZ)
        for coil in range(2):
            image = jnp.dot(edge_ref[coil], edge_rows, preferred_element_type=jnp.float32)
            for chunk, ref in enumerate((first_ref, second_ref)):
                rows = ref[:, 2 * pair + coil].reshape(depth, GZ)
                image = image + jnp.dot(main_ref[chunk], rows, preferred_element_type=jnp.float32)
            image_re, image_im = image[:GX], image[GX:]
            map_re = maps_ref[coil, 0].astype(jnp.float32)
            map_im = maps_ref[coil, 1].astype(jnp.float32)
            real = map_re * image_re + map_im * image_im
            imag = map_re * image_im - map_im * image_re
            total = [real, imag] if total[0] is None else [total[0] + real, total[1] + imag]
    for part in range(2):
        out_ref[:, part] = total[part].astype(jnp.bfloat16).reshape(8, GX // 8, GZ)


def combine(first, second, own, other):
    main_tab, edge_tab = x_tables()
    depth = GROUPS * 16
    maps = pl.BlockSpec((2, 2, GX, GZ), lambda y: (0, 0, 0, y))
    return pl.pallas_call(
        combine_kernel,
        grid=(2,),
        in_specs=[
            pl.BlockSpec((GROUPS, COILS, 16, GZ), lambda y: (0, 0, 0, y)),
            pl.BlockSpec((GROUPS, COILS + 2, 16, GZ), lambda y: (0, 0, 0, y)),
            pl.BlockSpec((CHUNKS, 2 * GX, depth), lambda y: (0, 0, 0)),
            pl.BlockSpec((2, 2 * GX, depth), lambda y: (0, 0, 0)),
            maps,
            maps,
        ],
        out_specs=pl.BlockSpec((8, 2, GX // 8, GZ), lambda y: (0, 0, 0, y)),
        out_shape=jax.ShapeDtypeStruct((8, 2, GX // 8, 2 * GZ), jnp.bfloat16),
        compiler_params=pltpu.CompilerParams(vmem_limit_bytes=36 * 2**20),
        cost_estimate=pl.CostEstimate(
            flops=2 * 4 * 2 * GX * 3 * depth * 2 * GZ, bytes_accessed=8 * 2**20, transcendentals=0
        ),
        name="combine",
    )(first, second, jnp.asarray(main_tab), jnp.asarray(edge_tab), own, other)


def pack_kernel(values_ref, offsets_ref, cells_ref, slots_ref, out_ref):
    used = slots_ref[...] < SLOTS
    cells = cells_ref[...]
    values = [values_ref[coil].astype(jnp.float32) for coil in range(2)]
    rows = [jnp.where(used, values[r // 2][r % 2 : r % 2 + 1], 0.0) for r in range(4)]
    spots = (cells // (GY * GZ), cells // GZ % GY, cells % GZ)
    first = lax.axis_index("core") == 0
    for axis in range(3):
        offset = offsets_ref[axis : axis + 1].astype(jnp.float32)
        rows.append(jnp.where(first, offset, spots[axis].astype(jnp.float32)))
    rows.append(jnp.zeros((1, SLOTS), jnp.float32))
    packed = jnp.concatenate(rows, 0).astype(jnp.bfloat16)
    width = BLOCKS * CAP
    for group in range(GROUPS):
        part = packed[:, group * width : (group + 1) * width]
        for copy in range(ZH):
            out_ref[copy * GROUPS + group] = part


def pack(values, offsets, cells, slots):
    return pl.pallas_call(
        pack_kernel,
        out_shape=jax.ShapeDtypeStruct((ZH * GROUPS, 8, BLOCKS * CAP), jnp.bfloat16),
        compiler_params=pltpu.CompilerParams(vmem_limit_bytes=56 * 2**20),
        name="pack",
    )(values, offsets, cells.reshape(1, SLOTS), slots.reshape(1, SLOTS))


def turn(array, axes):
    return lax.all_to_all(array, axes, split_axis=0, concat_axis=0, tiled=True)


def body(sample_values, sample_offsets, sample_cells, sample_slots, sensitivity):
    packed = pack(sample_values, sample_offsets, sample_cells, sample_slots)
    packed, sensitivity = lax.optimization_barrier((packed, sensitivity))
    planes = ("zl", "x", "core")
    got = turn(packed, ("zh",) + planes)
    samples = got.reshape(SOURCES, 16, BLOCKS * CAP)
    y_tab = lax.dynamic_index_in_dim(
        jnp.asarray(y_table()), lax.axis_index("zh"), 0, keepdims=False
    )
    z_tab = jnp.asarray(z_table())
    core = lax.axis_index("core")

    def maps(half):
        rows = lax.dynamic_slice_in_dim(sensitivity, 2 * half, 2, 3)
        return rows.reshape(2, 2, GX, 2 * GZ)

    other = lax.ppermute(maps(1 - core), "core", [(0, 1), (1, 0)])
    first, carry = grid_chunk(samples, y_tab, z_tab, 0)
    first = turn(first, planes)
    (second,) = grid_chunk(samples, y_tab, z_tab, 1, carry)
    partial = combine(first, turn(second, planes), maps(core), other)
    parts = turn(partial, ("y", "core")).reshape(4, 2, 2, GX // 8, 2, GZ)
    image = jnp.sum(parts.astype(jnp.float32), axis=0)
    return image.transpose(1, 2, 0, 3, 4).reshape(2, GX // 8, 4, GZ)


def solution(mesh):
    fine = Mesh(mesh.devices.reshape(8, 2, 4, 4, 2), ("zh", "zl", "x", "y", "core"))
    space, coil = ("zh", "zl", "x"), ("y", "core")
    placed = (
        P(coil, None, space),
        P(None, space),
        P(space),
        P(space),
        P(coil, None, None, space, None),
    )
    return jax.shard_map(
        body, mesh=fine, in_specs=placed, out_specs=P(None, coil, space, None), check_vma=False
    )
```

```python
import math

import jax
import jax.numpy as jnp
import ml_dtypes
import numpy as np
from jax import lax
from jax.experimental import pallas as pl
from jax.experimental.pallas import tpu as pltpu
from jax.sharding import Mesh
from jax.sharding import PartitionSpec as P

GX = 256
GY = 256
GZ = 256
SLOTS = 4096
CAP = 64

BETA = 9.0
TERMS = 31

ZH = 8
SOURCES = 64
UNIT = 16
GROUPS = 16
BLOCKS = 4
LANES = 256
STEP = 4
COILS = 4
ROWS = 32
TAPS = 4
SPAN = 7
PAIR = 2 * COILS * ROWS
HALF = PAIR // 2
CHUNKS = 2
PLANES = 8
HALO = 4


def series():
    quarter = 0.25 * BETA * BETA
    terms = [quarter**k / float(math.factorial(k)) ** 2 for k in range(TERMS)]
    total = math.fsum(terms)
    return [float(np.float32(t / total)) for t in terms]


def waves():
    counter = np.arange(256)
    phase = (counter[:, None] * counter[None, :] % 256).astype(np.float32) * np.float32(
        2.0 * math.pi / 256
    )
    scale = np.float32(1.0 / 16.0)
    both = np.stack([np.cos(phase) * scale, np.sin(phase) * scale], 0)
    return both.astype(ml_dtypes.bfloat16).astype(np.float32)


def z_table():
    cosine, sine = waves()
    return np.block([[cosine, sine], [-sine, cosine]]).astype(ml_dtypes.bfloat16)


def y_table():
    both = waves().reshape(2, ZH, ROWS, 256)
    return both.transpose(1, 0, 2, 3).reshape(ZH, 2 * ROWS, 256).astype(ml_dtypes.bfloat16)


def grid_table():
    rows = np.zeros((ZH, 2 * ROWS, 2 * GZ), ml_dtypes.bfloat16)
    rows[:, :, :GY] = y_table()
    return np.concatenate([rows, np.broadcast_to(z_table(), (ZH, 2 * GZ, 2 * GZ))], 1)


def x_columns(planes, part):
    cosine, sine = waves()
    if part == 0:
        return np.concatenate([cosine[:, planes], sine[:, planes]], 0)
    return np.concatenate([-sine[:, planes], cosine[:, planes]], 0)


def x_tables():
    main = []
    for chunk in range(CHUNKS):
        cols = []
        for group in range(GROUPS):
            planes = (16 * group + PLANES * chunk + np.arange(PLANES) - 1) % GX
            cols += [x_columns(planes, 0), x_columns(planes, 1)]
        main.append(np.concatenate(cols, 1))
    halo = []
    for coil in range(2):
        cols = []
        for group in range(GROUPS):
            planes = (16 * group + 16 + np.arange(HALO) - 1) % GX
            real = np.arange(HALO) < 3
            for other in range(2):
                keep = real & (other == coil)
                cols += [x_columns(planes, part) * keep for part in range(2)]
        halo.append(np.concatenate(cols, 1))
    return np.stack(main + halo).astype(ml_dtypes.bfloat16)


def tap_rows(first, second, lanes):
    row = lax.broadcasted_iota(jnp.int32, (8, lanes), 0)
    offset = jnp.where(row < TAPS, first, second)
    distance = offset + (1.0 - (row % TAPS).astype(jnp.float32))
    inner = jnp.maximum(1.0 - 0.25 * distance * distance, 0.0)
    coefficients = series()
    total = jnp.full((8, lanes), coefficients[-1], jnp.float32)
    for value in coefficients[-2::-1]:
        total = total * inner + value
    return total


def dense_rows(weights, base, lanes):
    high = base // 16
    low = base % 16
    row = lax.broadcasted_iota(jnp.int32, (16, lanes), 0)
    pattern = jnp.zeros((16, lanes), jnp.float32)
    for tap in range(TAPS):
        pattern = jnp.where(row == (low + tap) % 16, weights[tap], pattern)
    place = jnp.where(row < low, (high + 1) % 16, high).astype(jnp.float32)
    pattern = pattern.astype(jnp.bfloat16)
    place = place.astype(jnp.bfloat16)
    zero = jnp.zeros((16, lanes), jnp.bfloat16)
    return [
        jnp.where(place == jnp.bfloat16(block), pattern, zero) for block in range(16)
    ]


def build(packed, y_tab, pair_ref, dense_ref, at, lanes):
    taps_xy = tap_rows(packed[4:5], packed[5:6], lanes)
    taps_z = tap_rows(packed[6:7], packed[6:7], lanes)
    cell = packed.astype(jnp.int32)
    base_x = cell[12:13]
    base_y = (cell[13:14] + 255) % 256
    base_z = (cell[14:15] + 255) % 256
    z_blocks = dense_rows([taps_z[t : t + 1] for t in range(TAPS)], base_z, lanes)
    for block in range(16):
        dense_ref[block * 16 : (block + 1) * 16, at : at + lanes] = z_blocks[block]
    y_blocks = dense_rows([taps_xy[4 + t : 5 + t] for t in range(TAPS)], base_y, lanes)
    turn = jnp.dot(y_tab, jnp.concatenate(y_blocks, 0), preferred_element_type=jnp.float32)
    turn_re, turn_im = turn[:ROWS], turn[ROWS:]
    real, imag = [], []
    for coil in range(COILS):
        row = (coil // 2) * 8 + (coil % 2) * 2
        value_re, value_im = packed[row : row + 1], packed[row + 1 : row + 2]
        real.append((value_re * turn_re - value_im * turn_im).astype(jnp.bfloat16))
        imag.append((value_re * turn_im + value_im * turn_re).astype(jnp.bfloat16))
    values = real + imag
    row = lax.broadcasted_iota(jnp.int32, (8, lanes), 0)
    dense_x = jnp.zeros((8, lanes), jnp.float32)
    for tap in range(TAPS):
        dense_x = jnp.where(row == base_x + tap, taps_xy[tap : tap + 1], dense_x)
    for plane in range(SPAN):
        weight = jnp.broadcast_to(dense_x[plane : plane + 1], (ROWS, lanes)).astype(jnp.bfloat16)
        for part in range(2 * COILS):
            start = plane * PAIR + part * ROWS
            pair_ref[start : start + ROWS, at : at + lanes] = values[part] * weight


def transform_z(grid_planes, z_tab):
    planes = grid_planes.shape[0]
    grid = grid_planes.astype(jnp.bfloat16)
    joined = jnp.concatenate([grid[:, :HALF], grid[:, HALF:]], axis=2)
    along = jnp.dot(
        joined.reshape(planes * HALF, 2 * GZ), z_tab, preferred_element_type=jnp.float32
    )
    return jnp.swapaxes(along.reshape(planes, HALF, 2 * GZ), 0, 1)


def gather(samples_ref, start, offset):
    per = 128 // UNIT
    lane = lax.broadcasted_iota(jnp.int32, (16, 128), 1) // UNIT
    pieces = []
    for piece in range(LANES // 128):
        joined = None
        for k in range(per):
            rows = samples_ref[start + piece * per + k].astype(jnp.float32)
            rows = pltpu.roll(rows, (128 + UNIT * k - offset) % 128, 1)
            joined = rows if joined is None else jnp.where(lane == k, rows, joined)
        pieces.append(joined)
    return jnp.concatenate(pieces, 1)


def filled(samples_ref):
    def step(index, seen):
        return jnp.maximum(seen, jnp.abs(samples_ref[index].astype(jnp.float32)))

    seen = lax.fori_loop(0, SOURCES, step, jnp.zeros((16, 128), jnp.float32), unroll=8)
    row = lax.broadcasted_iota(jnp.int32, (16, 128), 0)
    seen = jnp.max(jnp.where(row % 8 < 4, seen, 0.0), axis=0, keepdims=True)
    seen = jnp.broadcast_to(seen, (8, 128))
    for shift in (8, 4, 2, 1):
        seen = jnp.maximum(seen, pltpu.roll(seen, shift, 1))
    lane = lax.broadcasted_iota(jnp.int32, (8, 128), 1)
    place = lax.broadcasted_iota(jnp.int32, (8, 128), 0)
    hit = (seen > 0.0) & (lane == place * UNIT + UNIT - 1)
    return jnp.sum(jnp.where(hit, (1 << place).astype(jnp.float32), 0.0)).astype(jnp.int32)


def grid_kernel(last, samples_ref, table_ref, *refs):
    if last:
        carry_ref, out_ref, pair_ref, dense_ref, acc_ref, list_ref = refs
    else:
        out_ref, carried_ref, pair_ref, dense_ref, acc_ref, list_ref = refs
    bits = filled(samples_ref)
    count = jnp.int32(0)
    for place in range(128 // UNIT):
        list_ref[count] = place
        count = count + ((bits >> place) & 1)
    if last:
        acc_ref[0:HALO] = carry_ref[...]
        acc_ref[HALO:] = jnp.zeros((PLANES, PAIR, GZ), jnp.float32)
    else:
        acc_ref[...] = jnp.zeros((PLANES + HALO, PAIR, GZ), jnp.float32)
    y_tab = table_ref[: 2 * ROWS, :GY]

    def step(index, _):
        block = list_ref[index]
        for part in range(STEP):
            packed = gather(samples_ref, part * (LANES // UNIT), block * UNIT)
            build(packed, y_tab, pair_ref, dense_ref, part * LANES, LANES)
        for plane in range(SPAN):
            product = lax.dot_general(
                pair_ref[plane * PAIR : (plane + 1) * PAIR],
                dense_ref[...],
                (((1,), (1,)), ((), ())),
                preferred_element_type=jnp.float32,
            )
            here = 4 * (block // (CAP // UNIT)) + plane
            acc_ref[here] = acc_ref[here] + product
        return 0

    lax.fori_loop(0, count, step, 0)

    z_tab = table_ref[2 * ROWS :]
    lines = transform_z(acc_ref[0:PLANES], z_tab)
    if last:
        edge = transform_z(acc_ref[PLANES:], z_tab)
    else:
        carried_ref[...] = acc_ref[PLANES:]
    for row in range(ROWS):
        owner = (row // 4) * 2 + row % 4 // 2
        here = slice(row % 2 * GZ, (row % 2 + 1) * GZ)
        for coil in range(COILS):
            line = lines[coil * ROWS + row]
            out_ref[owner, coil, :, here] = jnp.concatenate([line[:, :GZ], line[:, GZ:]], 0).astype(
                jnp.bfloat16
            )
        for pair in range(COILS // 2) if last else ():
            pieces = []
            for inner in range(2):
                line = edge[(2 * pair + inner) * ROWS + row]
                pieces += [line[:, :GZ], line[:, GZ:]]
            out_ref[owner, COILS + pair, :, here] = jnp.concatenate(pieces, 0).astype(jnp.bfloat16)


def grid_chunk(samples, table, chunk, carry=None):
    last = carry is not None
    tiles = COILS + (COILS // 2 if last else 0)
    flops = 2 * SPAN * PAIR * GZ * SOURCES * CAP * BLOCKS // CHUNKS
    edges = (HALO, PAIR, GZ)
    in_specs = [
        pl.BlockSpec((SOURCES, 16, 128), lambda q: (0, 0, chunk)),
        pl.BlockSpec((2 * ROWS + 2 * GZ, 2 * GZ), lambda q: (0, 0)),
    ]
    out_specs = [pl.BlockSpec((GROUPS, tiles, 16, 2 * GZ), lambda q: (0, 0, 0, 0))]
    out_shape = [jax.ShapeDtypeStruct((GROUPS, tiles, 16, 2 * GZ), jnp.bfloat16)]
    operands = [samples, table]
    if last:
        in_specs.append(pl.BlockSpec(edges, lambda q: (0, 0, 0)))
        operands.append(carry)
    else:
        out_specs.append(pl.BlockSpec(edges, lambda q: (0, 0, 0)))
        out_shape.append(jax.ShapeDtypeStruct(edges, jnp.float32))
    return pl.pallas_call(
        lambda *refs: grid_kernel(last, *refs),
        grid=(1,),
        in_specs=in_specs,
        out_specs=out_specs,
        out_shape=out_shape,
        scratch_shapes=[
            pltpu.VMEM((SPAN * PAIR, STEP * LANES), jnp.bfloat16),
            pltpu.VMEM((GZ, STEP * LANES), jnp.bfloat16),
            pltpu.VMEM((PLANES + HALO, PAIR, GZ), jnp.float32),
            pltpu.SMEM((9,), jnp.int32),
        ],
        compiler_params=pltpu.CompilerParams(vmem_limit_bytes=36 * 2**20),
        cost_estimate=pl.CostEstimate(flops=flops, bytes_accessed=4 * 2**20, transcendentals=0),
        name="grid_chunk",
    )(*operands)


def combine_kernel(first_ref, second_ref, table_ref, own_hbm, other_hbm, out_ref, own_ref, other_ref, sems):
    copies = [
        pltpu.make_async_copy(own_hbm, own_ref, sems.at[0]),
        pltpu.make_async_copy(other_hbm, other_ref, sems.at[1]),
    ]
    for copy in copies:
        copy.start()
    core = lax.axis_index("core")
    depth = GROUPS * 16
    for e in range(2):
        lanes = slice(e * GZ, (e + 1) * GZ)
        total = None
        for side, (maps_ref, pair) in enumerate(((own_ref, core), (other_ref, 1 - core))):
            edge_rows = second_ref[:, COILS + pair, :, lanes].reshape(depth, GZ)
            for coil in range(2):
                image = jnp.dot(
                    table_ref[CHUNKS + coil], edge_rows, preferred_element_type=jnp.float32
                )
                for chunk, ref in enumerate((first_ref, second_ref)):
                    rows = ref[:, 2 * pair + coil, :, lanes].reshape(depth, GZ)
                    image = image + jnp.dot(
                        table_ref[chunk], rows, preferred_element_type=jnp.float32
                    )
                if e == coil == 0:
                    copies[side].wait()
                image_re, image_im = image[:GX], image[GX:]
                map_re = maps_ref[coil, 0, :, lanes].astype(jnp.float32)
                map_im = maps_ref[coil, 1, :, lanes].astype(jnp.float32)
                real = map_re * image_re + map_im * image_im
                imag = map_re * image_im - map_im * image_re
                total = [real, imag] if total is None else [total[0] + real, total[1] + imag]
        for part in range(2):
            out_ref[:, part, :, lanes] = total[part].astype(jnp.bfloat16).reshape(8, GX // 8, GZ)


def combine(first, second, table, own, other):
    vmem, hbm = pl.BlockSpec(memory_space=pltpu.VMEM), pl.BlockSpec(memory_space=pltpu.HBM)
    return pl.pallas_call(
        combine_kernel,
        in_specs=[vmem, vmem, vmem, hbm, hbm],
        out_specs=vmem,
        out_shape=jax.ShapeDtypeStruct((8, 2, GX // 8, 2 * GZ), jnp.bfloat16),
        scratch_shapes=[
            pltpu.VMEM((2, 2, GX, 2 * GZ), jnp.bfloat16),
            pltpu.VMEM((2, 2, GX, 2 * GZ), jnp.bfloat16),
            pltpu.SemaphoreType.DMA((2,)),
        ],
        compiler_params=pltpu.CompilerParams(vmem_limit_bytes=36 * 2**20),
        cost_estimate=pl.CostEstimate(
            flops=2 * 4 * 2 * GX * 3 * GROUPS * 16 * 2 * GZ,
            bytes_accessed=8 * 2**20,
            transcendentals=0,
        ),
        name="combine",
    )(first, second, table, own, other)


def add_kernel(parts_ref, out_ref):
    for half in range(2):
        total = parts_ref[half].astype(jnp.float32)
        for chip in range(1, 4):
            total = total + parts_ref[2 * chip + half].astype(jnp.float32)
        for e in range(2):
            for part in range(2):
                out_ref[part, :, 2 * half + e, :] = total[part, :, e * GZ : (e + 1) * GZ]


def add(parts):
    return pl.pallas_call(
        add_kernel,
        out_shape=jax.ShapeDtypeStruct((2, GX // 8, 4, GZ), jnp.float32),
        compiler_params=pltpu.CompilerParams(vmem_limit_bytes=16 * 2**20),
        name="add",
    )(parts)


def pack_kernel(values_ref, offsets_ref, cells_ref, slots_ref, out_ref):
    used = slots_ref[...] < SLOTS
    cells = cells_ref[...]
    values = [values_ref[coil].astype(jnp.float32) for coil in range(2)]
    rows = [jnp.where(used, values[r // 2][r % 2 : r % 2 + 1], 0.0) for r in range(4)]
    spots = (cells // (GY * GZ), cells // GZ % GY, cells % GZ)
    first = lax.axis_index("core") == 0
    for axis in range(3):
        offset = offsets_ref[axis : axis + 1].astype(jnp.float32)
        rows.append(jnp.where(first, offset, spots[axis].astype(jnp.float32)))
    rows.append(jnp.zeros((1, SLOTS), jnp.float32))
    packed = jnp.concatenate(rows, 0).astype(jnp.bfloat16)
    width = BLOCKS * CAP
    for group in range(GROUPS):
        part = packed[:, group * width : (group + 1) * width]
        for copy in range(ZH):
            out_ref[copy * GROUPS + group] = part


def pack(values, offsets, cells, slots):
    return pl.pallas_call(
        pack_kernel,
        out_shape=jax.ShapeDtypeStruct((ZH * GROUPS, 8, BLOCKS * CAP), jnp.bfloat16),
        compiler_params=pltpu.CompilerParams(vmem_limit_bytes=56 * 2**20),
        name="pack",
    )(values, offsets, cells.reshape(1, SLOTS), slots.reshape(1, SLOTS))


def turn(array, axes):
    return lax.all_to_all(array, axes, split_axis=0, concat_axis=0, tiled=True)


def body(sample_values, sample_offsets, sample_cells, sample_slots, sensitivity):
    packed = pack(sample_values, sample_offsets, sample_cells, sample_slots)
    packed, sensitivity = lax.optimization_barrier((packed, sensitivity))
    planes = ("zl", "x", "core")
    got = turn(packed, ("zh",) + planes)
    samples = got.reshape(SOURCES, 16, BLOCKS * CAP)

    def pick(tables, axis):
        here = lax.axis_index(axis)
        return lax.dynamic_index_in_dim(jnp.asarray(tables), here, 0, keepdims=False)

    table = pick(grid_table(), "zh")
    core = lax.axis_index("core")

    def maps(half):
        rows = lax.dynamic_slice_in_dim(sensitivity, 2 * half, 2, 3)
        return rows.reshape(2, 2, GX, 2 * GZ)

    other = lax.ppermute(maps(1 - core), "core", [(0, 1), (1, 0)])
    first, carry = grid_chunk(samples, table, 0)
    first = turn(first, planes)
    (second,) = grid_chunk(samples, table, 1, carry)
    both = np.broadcast_to(x_tables()[None], (2, CHUNKS + 2, 2 * GX, GROUPS * 16))
    partial = combine(first, turn(second, planes), pick(both, "core"), maps(core), other)
    return add(turn(partial, ("y", "core")))


def solution(mesh):
    fine = Mesh(mesh.devices.reshape(8, 2, 4, 4, 2), ("zh", "zl", "x", "y", "core"))
    space, coil = ("zh", "zl", "x"), ("y", "core")
    placed = (
        P(coil, None, space),
        P(None, space),
        P(space),
        P(space),
        P(coil, None, None, space, None),
    )
    return jax.shard_map(
        body, mesh=fine, in_specs=placed, out_specs=P(None, coil, space, None), check_vma=False
    )
```

```python
import math

import jax
import jax.numpy as jnp
import ml_dtypes
import numpy as np
from jax import lax
from jax.experimental import pallas as pl
from jax.experimental.pallas import tpu as pltpu
from jax.sharding import Mesh
from jax.sharding import PartitionSpec as P

GX = 256
GY = 256
GZ = 256
SLOTS = 4096
CAP = 64

BETA = 9.0
TERMS = 31

ZH = 8
SOURCES = 64
UNIT = 16
GROUPS = 16
BLOCKS = 4
LANES = 256
STEP = 4
COILS = 4
ROWS = 32
TAPS = 4
SPAN = 7
PAIR = 2 * COILS * ROWS
HALF = PAIR // 2
CHUNKS = 2
PLANES = 8
EDGE = 3


def series():
    quarter = 0.25 * BETA * BETA
    terms = [quarter**k / float(math.factorial(k)) ** 2 for k in range(TERMS)]
    total = math.fsum(terms)
    return [float(np.float32(t / total)) for t in terms]


def waves():
    counter = np.arange(256)
    phase = (counter[:, None] * counter[None, :] % 256).astype(np.float32) * np.float32(
        2.0 * math.pi / 256
    )
    scale = np.float32(1.0 / 16.0)
    both = np.stack([np.cos(phase) * scale, np.sin(phase) * scale], 0)
    return both.astype(ml_dtypes.bfloat16).astype(np.float32)


def z_table():
    cosine, sine = waves()
    return np.block([[cosine, sine], [-sine, cosine]]).astype(ml_dtypes.bfloat16)


def y_table():
    both = waves().reshape(2, ZH, ROWS, 256)
    return both.transpose(1, 0, 2, 3).reshape(ZH, 2 * ROWS, 256).astype(ml_dtypes.bfloat16)


def grid_table():
    rows = np.zeros((ZH, 2 * ROWS, 2 * GZ), ml_dtypes.bfloat16)
    rows[:, :, :GY] = y_table()
    return np.concatenate([rows, np.broadcast_to(z_table(), (ZH, 2 * GZ, 2 * GZ))], 1)


def x_columns(planes, part):
    cosine, sine = waves()
    if part == 0:
        return np.concatenate([cosine[:, planes], sine[:, planes]], 0)
    return np.concatenate([-sine[:, planes], cosine[:, planes]], 0)


def x_tables():
    main = []
    for first in (PLANES + EDGE, 0):
        cols = []
        for group in range(GROUPS):
            planes = (16 * group + first + np.arange(PLANES) - 1) % GX
            cols += [x_columns(planes, 0), x_columns(planes, 1)]
        main.append(np.concatenate(cols, 1))
    edge = []
    for coil in range(2):
        cols = []
        for group in range(GROUPS):
            planes = (16 * group + PLANES + np.arange(EDGE + 1) - 1) % GX
            real = np.arange(EDGE + 1) < EDGE
            for other in range(2):
                keep = real & (other == coil)
                cols += [x_columns(planes, part) * keep for part in range(2)]
        edge.append(np.concatenate(cols, 1))
    return np.stack(main + edge).astype(ml_dtypes.bfloat16)


def tap_rows(first, second, lanes):
    row = lax.broadcasted_iota(jnp.int32, (8, lanes), 0)
    offset = jnp.where(row < TAPS, first, second)
    distance = offset + (1.0 - (row % TAPS).astype(jnp.float32))
    inner = jnp.maximum(1.0 - 0.25 * distance * distance, 0.0)
    coefficients = series()
    total = jnp.full((8, lanes), coefficients[-1], jnp.float32)
    for value in coefficients[-2::-1]:
        total = total * inner + value
    return total


def dense_rows(weights, base, lanes):
    high = base // 16
    low = base % 16
    row = lax.broadcasted_iota(jnp.int32, (16, lanes), 0)
    pattern = jnp.zeros((16, lanes), jnp.float32)
    for tap in range(TAPS):
        pattern = jnp.where(row == (low + tap) % 16, weights[tap], pattern)
    place = jnp.where(row < low, (high + 1) % 16, high).astype(jnp.float32)
    pattern = pattern.astype(jnp.bfloat16)
    place = place.astype(jnp.bfloat16)
    zero = jnp.zeros((16, lanes), jnp.bfloat16)
    return [
        jnp.where(place == jnp.bfloat16(block), pattern, zero) for block in range(16)
    ]


def build(packed, y_tab, pair_ref, dense_ref, at, lanes):
    taps_xy = tap_rows(packed[4:5], packed[5:6], lanes)
    taps_z = tap_rows(packed[6:7], packed[6:7], lanes)
    cell = packed.astype(jnp.int32)
    base_x = cell[12:13]
    base_y = (cell[13:14] + 255) % 256
    base_z = (cell[14:15] + 255) % 256
    z_blocks = dense_rows([taps_z[t : t + 1] for t in range(TAPS)], base_z, lanes)
    for block in range(16):
        dense_ref[block * 16 : (block + 1) * 16, at : at + lanes] = z_blocks[block]
    y_blocks = dense_rows([taps_xy[4 + t : 5 + t] for t in range(TAPS)], base_y, lanes)
    turn = jnp.dot(y_tab, jnp.concatenate(y_blocks, 0), preferred_element_type=jnp.float32)
    turn_re, turn_im = turn[:ROWS], turn[ROWS:]
    real, imag = [], []
    for coil in range(COILS):
        row = (coil // 2) * 8 + (coil % 2) * 2
        value_re, value_im = packed[row : row + 1], packed[row + 1 : row + 2]
        real.append((value_re * turn_re - value_im * turn_im).astype(jnp.bfloat16))
        imag.append((value_re * turn_im + value_im * turn_re).astype(jnp.bfloat16))
    values = real + imag
    row = lax.broadcasted_iota(jnp.int32, (8, lanes), 0)
    dense_x = jnp.zeros((8, lanes), jnp.float32)
    for tap in range(TAPS):
        dense_x = jnp.where(row == base_x + tap, taps_xy[tap : tap + 1], dense_x)
    for plane in range(SPAN):
        weight = jnp.broadcast_to(dense_x[plane : plane + 1], (ROWS, lanes)).astype(jnp.bfloat16)
        for part in range(2 * COILS):
            start = plane * PAIR + part * ROWS
            pair_ref[start : start + ROWS, at : at + lanes] = values[part] * weight


def transform_z(grid_planes, z_tab):
    planes = grid_planes.shape[0]
    grid = grid_planes.astype(jnp.bfloat16)
    joined = jnp.concatenate([grid[:, :HALF], grid[:, HALF:]], axis=2)
    along = jnp.dot(
        joined.reshape(planes * HALF, 2 * GZ), z_tab, preferred_element_type=jnp.float32
    )
    return jnp.swapaxes(along.reshape(planes, HALF, 2 * GZ), 0, 1)


def gather(samples_ref, start, offset):
    per = 128 // UNIT
    lane = lax.broadcasted_iota(jnp.int32, (16, 128), 1) // UNIT
    pieces = []
    for piece in range(LANES // 128):
        joined = None
        for k in range(per):
            rows = samples_ref[start + piece * per + k].astype(jnp.float32)
            rows = pltpu.roll(rows, (128 + UNIT * k - offset) % 128, 1)
            joined = rows if joined is None else jnp.where(lane == k, rows, joined)
        pieces.append(joined)
    return jnp.concatenate(pieces, 1)


def filled(samples_ref):
    def step(index, seen):
        return jnp.maximum(seen, jnp.abs(samples_ref[index].astype(jnp.float32)))

    seen = lax.fori_loop(0, SOURCES, step, jnp.zeros((16, 128), jnp.float32), unroll=8)
    row = lax.broadcasted_iota(jnp.int32, (16, 128), 0)
    seen = jnp.max(jnp.where(row % 8 < 4, seen, 0.0), axis=0, keepdims=True)
    seen = jnp.broadcast_to(seen, (8, 128))
    for shift in (8, 4, 2, 1):
        seen = jnp.maximum(seen, pltpu.roll(seen, shift, 1))
    lane = lax.broadcasted_iota(jnp.int32, (8, 128), 1)
    place = lax.broadcasted_iota(jnp.int32, (8, 128), 0)
    hit = (seen > 0.0) & (lane == place * UNIT + UNIT - 1)
    return jnp.sum(jnp.where(hit, (1 << place).astype(jnp.float32), 0.0)).astype(jnp.int32)


def grid_kernel(last, samples_ref, table_ref, *refs):
    if last:
        carry_ref, out_ref, pair_ref, dense_ref, acc_ref, list_ref = refs
    else:
        out_ref, carried_ref, pair_ref, dense_ref, acc_ref, list_ref = refs
    bits = filled(samples_ref)
    count = jnp.int32(0)
    for place in range(128 // UNIT):
        list_ref[count] = place
        count = count + ((bits >> place) & 1)
    acc_ref[...] = jnp.zeros(acc_ref.shape, jnp.float32)
    if last:
        acc_ref[PLANES : PLANES + EDGE] = carry_ref[...]
    y_tab = table_ref[: 2 * ROWS, :GY]

    def step(index, _):
        block = list_ref[index]
        for part in range(STEP):
            packed = gather(samples_ref, part * (LANES // UNIT), block * UNIT)
            build(packed, y_tab, pair_ref, dense_ref, part * LANES, LANES)
        for plane in range(SPAN):
            product = lax.dot_general(
                pair_ref[plane * PAIR : (plane + 1) * PAIR],
                dense_ref[...],
                (((1,), (1,)), ((), ())),
                preferred_element_type=jnp.float32,
            )
            here = 4 * (block // (CAP // UNIT)) + plane
            acc_ref[here] = acc_ref[here] + product
        return 0

    lax.fori_loop(0, count, step, 0)

    z_tab = table_ref[2 * ROWS :]
    if last:
        lines = transform_z(acc_ref[0:PLANES], z_tab)
        edge = transform_z(acc_ref[PLANES:], z_tab)
    else:
        lines = transform_z(acc_ref[EDGE : EDGE + PLANES], z_tab)
        carried_ref[...] = acc_ref[0:EDGE]
    for row in range(ROWS):
        owner = (row // 4) * 2 + row % 4 // 2
        here = slice(row % 2 * GZ, (row % 2 + 1) * GZ)
        for coil in range(COILS):
            line = lines[coil * ROWS + row]
            out_ref[owner, coil, :, here] = jnp.concatenate([line[:, :GZ], line[:, GZ:]], 0).astype(
                jnp.bfloat16
            )
        for pair in range(COILS // 2) if last else ():
            pieces = []
            for inner in range(2):
                line = edge[(2 * pair + inner) * ROWS + row]
                pieces += [line[:, :GZ], line[:, GZ:]]
            out_ref[owner, COILS + pair, :, here] = jnp.concatenate(pieces, 0).astype(jnp.bfloat16)


def grid_chunk(samples, table, chunk, carry=None):
    last = carry is not None
    tiles = COILS + (COILS // 2 if last else 0)
    flops = 2 * SPAN * PAIR * GZ * SOURCES * CAP * BLOCKS // CHUNKS
    edges = (EDGE, PAIR, GZ)
    in_specs = [
        pl.BlockSpec((SOURCES, 16, 128), lambda q: (0, 0, CHUNKS - 1 - chunk)),
        pl.BlockSpec((2 * ROWS + 2 * GZ, 2 * GZ), lambda q: (0, 0)),
    ]
    out_specs = [pl.BlockSpec((GROUPS, tiles, 16, 2 * GZ), lambda q: (0, 0, 0, 0))]
    out_shape = [jax.ShapeDtypeStruct((GROUPS, tiles, 16, 2 * GZ), jnp.bfloat16)]
    operands = [samples, table]
    if last:
        in_specs.append(pl.BlockSpec(edges, lambda q: (0, 0, 0)))
        operands.append(carry)
    else:
        out_specs.append(pl.BlockSpec(edges, lambda q: (0, 0, 0)))
        out_shape.append(jax.ShapeDtypeStruct(edges, jnp.float32))
    return pl.pallas_call(
        lambda *refs: grid_kernel(last, *refs),
        grid=(1,),
        in_specs=in_specs,
        out_specs=out_specs,
        out_shape=out_shape,
        scratch_shapes=[
            pltpu.VMEM((SPAN * PAIR, STEP * LANES), jnp.bfloat16),
            pltpu.VMEM((GZ, STEP * LANES), jnp.bfloat16),
            pltpu.VMEM((PLANES + EDGE + 1, PAIR, GZ), jnp.float32),
            pltpu.SMEM((9,), jnp.int32),
        ],
        compiler_params=pltpu.CompilerParams(vmem_limit_bytes=36 * 2**20),
        cost_estimate=pl.CostEstimate(flops=flops, bytes_accessed=4 * 2**20, transcendentals=0),
        name="grid_chunk",
    )(*operands)


def combine_kernel(first_ref, second_ref, table_ref, own_hbm, other_hbm, out_ref, own_ref, other_ref, sems):
    copies = [
        pltpu.make_async_copy(own_hbm, own_ref, sems.at[0]),
        pltpu.make_async_copy(other_hbm, other_ref, sems.at[1]),
    ]
    for copy in copies:
        copy.start()
    core = lax.axis_index("core")
    depth = GROUPS * 16
    for e in range(2):
        lanes = slice(e * GZ, (e + 1) * GZ)
        total = None
        for side, (maps_ref, pair) in enumerate(((own_ref, core), (other_ref, 1 - core))):
            edge_rows = second_ref[:, COILS + pair, :, lanes].reshape(depth, GZ)
            for coil in range(2):
                image = jnp.dot(
                    table_ref[CHUNKS + coil], edge_rows, preferred_element_type=jnp.float32
                )
                for chunk, ref in enumerate((first_ref, second_ref)):
                    rows = ref[:, 2 * pair + coil, :, lanes].reshape(depth, GZ)
                    image = image + jnp.dot(
                        table_ref[chunk], rows, preferred_element_type=jnp.float32
                    )
                if e == coil == 0:
                    copies[side].wait()
                image_re, image_im = image[:GX], image[GX:]
                map_re = maps_ref[coil, 0, :, lanes].astype(jnp.float32)
                map_im = maps_ref[coil, 1, :, lanes].astype(jnp.float32)
                real = map_re * image_re + map_im * image_im
                imag = map_re * image_im - map_im * image_re
                total = [real, imag] if total is None else [total[0] + real, total[1] + imag]
        for part in range(2):
            out_ref[:, part, :, lanes] = total[part].astype(jnp.bfloat16).reshape(8, GX // 8, GZ)


def combine(first, second, table, own, other):
    vmem, hbm = pl.BlockSpec(memory_space=pltpu.VMEM), pl.BlockSpec(memory_space=pltpu.HBM)
    return pl.pallas_call(
        combine_kernel,
        in_specs=[vmem, vmem, vmem, hbm, hbm],
        out_specs=vmem,
        out_shape=jax.ShapeDtypeStruct((8, 2, GX // 8, 2 * GZ), jnp.bfloat16),
        scratch_shapes=[
            pltpu.VMEM((2, 2, GX, 2 * GZ), jnp.bfloat16),
            pltpu.VMEM((2, 2, GX, 2 * GZ), jnp.bfloat16),
            pltpu.SemaphoreType.DMA((2,)),
        ],
        compiler_params=pltpu.CompilerParams(vmem_limit_bytes=36 * 2**20),
        cost_estimate=pl.CostEstimate(
            flops=2 * 4 * 2 * GX * 3 * GROUPS * 16 * 2 * GZ,
            bytes_accessed=8 * 2**20,
            transcendentals=0,
        ),
        name="combine",
    )(first, second, table, own, other)


def add_kernel(parts_ref, out_ref):
    for half in range(2):
        total = parts_ref[half].astype(jnp.float32)
        for chip in range(1, 4):
            total = total + parts_ref[2 * chip + half].astype(jnp.float32)
        for e in range(2):
            for part in range(2):
                out_ref[part, :, 2 * half + e, :] = total[part, :, e * GZ : (e + 1) * GZ]


def add(parts):
    return pl.pallas_call(
        add_kernel,
        out_shape=jax.ShapeDtypeStruct((2, GX // 8, 4, GZ), jnp.float32),
        compiler_params=pltpu.CompilerParams(vmem_limit_bytes=16 * 2**20),
        name="add",
    )(parts)


def pack_kernel(values_ref, offsets_ref, cells_ref, slots_ref, out_ref):
    used = slots_ref[...] < SLOTS
    cells = cells_ref[...]
    values = [values_ref[coil].astype(jnp.float32) for coil in range(2)]
    rows = [jnp.where(used, values[r // 2][r % 2 : r % 2 + 1], 0.0) for r in range(4)]
    spots = (cells // (GY * GZ), cells // GZ % GY, cells % GZ)
    first = lax.axis_index("core") == 0
    for axis in range(3):
        offset = offsets_ref[axis : axis + 1].astype(jnp.float32)
        rows.append(jnp.where(first, offset, spots[axis].astype(jnp.float32)))
    rows.append(jnp.zeros((1, SLOTS), jnp.float32))
    packed = jnp.concatenate(rows, 0).astype(jnp.bfloat16)
    width = BLOCKS * CAP
    for group in range(GROUPS):
        part = packed[:, group * width : (group + 1) * width]
        for copy in range(ZH):
            out_ref[copy * GROUPS + group] = part


def pack(values, offsets, cells, slots):
    return pl.pallas_call(
        pack_kernel,
        out_shape=jax.ShapeDtypeStruct((ZH * GROUPS, 8, BLOCKS * CAP), jnp.bfloat16),
        compiler_params=pltpu.CompilerParams(vmem_limit_bytes=56 * 2**20),
        name="pack",
    )(values, offsets, cells.reshape(1, SLOTS), slots.reshape(1, SLOTS))


def turn(array, axes):
    return lax.all_to_all(array, axes, split_axis=0, concat_axis=0, tiled=True)


def body(sample_values, sample_offsets, sample_cells, sample_slots, sensitivity):
    packed = pack(sample_values, sample_offsets, sample_cells, sample_slots)
    packed, sensitivity = lax.optimization_barrier((packed, sensitivity))
    planes = ("zl", "x", "core")
    got = turn(packed, ("zh",) + planes)
    samples = got.reshape(SOURCES, 16, BLOCKS * CAP)

    def pick(tables, axis):
        here = lax.axis_index(axis)
        return lax.dynamic_index_in_dim(jnp.asarray(tables), here, 0, keepdims=False)

    table = pick(grid_table(), "zh")
    core = lax.axis_index("core")

    def maps(half):
        rows = lax.dynamic_slice_in_dim(sensitivity, 2 * half, 2, 3)
        return rows.reshape(2, 2, GX, 2 * GZ)

    other = lax.ppermute(maps(1 - core), "core", [(0, 1), (1, 0)])
    first, carry = grid_chunk(samples, table, 0)
    first = turn(first, planes)
    (second,) = grid_chunk(samples, table, 1, carry)
    both = np.broadcast_to(x_tables()[None], (2, CHUNKS + 2, 2 * GX, GROUPS * 16))
    partial = combine(first, turn(second, planes), pick(both, "core"), maps(core), other)
    return add(turn(partial, ("y", "core")))


def solution(mesh):
    fine = Mesh(mesh.devices.reshape(8, 2, 4, 4, 2), ("zh", "zl", "x", "y", "core"))
    space, coil = ("zh", "zl", "x"), ("y", "core")
    placed = (
        P(coil, None, space),
        P(None, space),
        P(space),
        P(space),
        P(coil, None, None, space, None),
    )
    return jax.shard_map(
        body, mesh=fine, in_specs=placed, out_specs=P(None, coil, space, None), check_vma=False
    )
```

```python
import math

import jax
import jax.numpy as jnp
import ml_dtypes
import numpy as np
from jax import lax
from jax.experimental import pallas as pl
from jax.experimental.pallas import tpu as pltpu
from jax.sharding import Mesh
from jax.sharding import PartitionSpec as P

GX = 256
GY = 256
GZ = 256
SLOTS = 4096
CAP = 64

BETA = 9.0
TERMS = 31

ZH = 8
SOURCES = 64
UNIT = 16
GROUPS = 16
BLOCKS = 4
LANES = 256
STEP = 4
COILS = 4
ROWS = 32
TAPS = 4
SPAN = 7
PAIR = 2 * COILS * ROWS
HALF = PAIR // 2
CHUNKS = 2
PLANES = 8
EDGE = 3


def series():
    quarter = 0.25 * BETA * BETA
    terms = [quarter**k / float(math.factorial(k)) ** 2 for k in range(TERMS)]
    total = math.fsum(terms)
    return [float(np.float32(t / total)) for t in terms]


def waves():
    counter = np.arange(256)
    phase = (counter[:, None] * counter[None, :] % 256).astype(np.float32) * np.float32(
        2.0 * math.pi / 256
    )
    scale = np.float32(1.0 / 16.0)
    both = np.stack([np.cos(phase) * scale, np.sin(phase) * scale], 0)
    return both.astype(ml_dtypes.bfloat16).astype(np.float32)


def z_table():
    cosine, sine = waves()
    return np.block([[cosine, sine], [-sine, cosine]]).astype(ml_dtypes.bfloat16)


def y_table():
    both = waves().reshape(2, ZH, ROWS, 256)
    return both.transpose(1, 0, 2, 3).reshape(ZH, 2 * ROWS, 256).astype(ml_dtypes.bfloat16)


def grid_table():
    rows = np.zeros((ZH, 2 * ROWS, 2 * GZ), ml_dtypes.bfloat16)
    rows[:, :, :GY] = y_table()
    return np.concatenate([rows, np.broadcast_to(z_table(), (ZH, 2 * GZ, 2 * GZ))], 1)


def x_columns(planes, part):
    cosine, sine = waves()
    if part == 0:
        return np.concatenate([cosine[:, planes], sine[:, planes]], 0)
    return np.concatenate([-sine[:, planes], cosine[:, planes]], 0)


def x_tables():
    main = []
    for first in (PLANES + EDGE, 0):
        cols = []
        for group in range(GROUPS):
            planes = (16 * group + first + np.arange(PLANES) - 1) % GX
            cols += [x_columns(planes, 0), x_columns(planes, 1)]
        main.append(np.concatenate(cols, 1))
    edge = []
    for coil in range(2):
        cols = []
        for group in range(GROUPS):
            planes = (16 * group + PLANES + np.arange(EDGE + 1) - 1) % GX
            real = np.arange(EDGE + 1) < EDGE
            for other in range(2):
                keep = real & (other == coil)
                cols += [x_columns(planes, part) * keep for part in range(2)]
        edge.append(np.concatenate(cols, 1))
    return np.stack(main + edge).astype(ml_dtypes.bfloat16)


def tap_rows(first, second, lanes):
    row = lax.broadcasted_iota(jnp.int32, (8, lanes), 0)
    offset = jnp.where(row < TAPS, first, second)
    distance = offset + (1.0 - (row % TAPS).astype(jnp.float32))
    inner = jnp.maximum(1.0 - 0.25 * distance * distance, 0.0)
    coefficients = series()
    total = jnp.full((8, lanes), coefficients[-1], jnp.float32)
    for value in coefficients[-2::-1]:
        total = total * inner + value
    return total


def dense_rows(weights, base, lanes):
    high = base // 16
    low = base % 16
    row = lax.broadcasted_iota(jnp.int32, (16, lanes), 0)
    pattern = jnp.zeros((16, lanes), jnp.float32)
    for tap in range(TAPS):
        pattern = jnp.where(row == (low + tap) % 16, weights[tap], pattern)
    place = jnp.where(row < low, (high + 1) % 16, high).astype(jnp.float32)
    pattern = pattern.astype(jnp.bfloat16)
    place = place.astype(jnp.bfloat16)
    zero = jnp.zeros((16, lanes), jnp.bfloat16)
    return [
        jnp.where(place == jnp.bfloat16(block), pattern, zero) for block in range(16)
    ]


def build(packed, y_tab, pair_ref, dense_ref, at, lanes):
    taps_xy = tap_rows(packed[4:5], packed[5:6], lanes)
    taps_z = tap_rows(packed[6:7], packed[6:7], lanes)
    cell = packed.astype(jnp.int32)
    base_x = cell[12:13]
    base_y = (cell[13:14] + 255) % 256
    base_z = (cell[14:15] + 255) % 256
    z_blocks = dense_rows([taps_z[t : t + 1] for t in range(TAPS)], base_z, lanes)
    for block in range(16):
        dense_ref[block * 16 : (block + 1) * 16, at : at + lanes] = z_blocks[block]
    y_blocks = dense_rows([taps_xy[4 + t : 5 + t] for t in range(TAPS)], base_y, lanes)
    turn = jnp.dot(y_tab, jnp.concatenate(y_blocks, 0), preferred_element_type=jnp.float32)
    turn_re, turn_im = turn[:ROWS], turn[ROWS:]
    real, imag = [], []
    for coil in range(COILS):
        row = (coil // 2) * 8 + (coil % 2) * 2
        value_re, value_im = packed[row : row + 1], packed[row + 1 : row + 2]
        real.append(value_re * turn_re - value_im * turn_im)
        imag.append(value_re * turn_im + value_im * turn_re)
    values = real + imag
    row = lax.broadcasted_iota(jnp.int32, (8, lanes), 0)
    dense_x = jnp.zeros((8, lanes), jnp.float32)
    for tap in range(TAPS):
        dense_x = jnp.where(row == base_x + tap, taps_xy[tap : tap + 1], dense_x)
    for plane in range(SPAN):
        weight = dense_x[plane : plane + 1]
        for part in range(2 * COILS):
            start = plane * PAIR + part * ROWS
            pair_ref[start : start + ROWS, at : at + lanes] = (values[part] * weight).astype(
                jnp.bfloat16
            )


def transform_z(grid_planes, z_tab):
    planes = grid_planes.shape[0]
    grid = grid_planes.astype(jnp.bfloat16)
    joined = jnp.concatenate([grid[:, :HALF], grid[:, HALF:]], axis=2)
    along = jnp.dot(
        joined.reshape(planes * HALF, 2 * GZ), z_tab, preferred_element_type=jnp.float32
    )
    return jnp.swapaxes(along.reshape(planes, HALF, 2 * GZ), 0, 1)


def gather(samples_ref, start, offset):
    per = 128 // UNIT
    lane = lax.broadcasted_iota(jnp.int32, (16, 128), 1) // UNIT
    pieces = []
    for piece in range(LANES // 128):
        joined = None
        for k in range(per):
            rows = samples_ref[start + piece * per + k].astype(jnp.float32)
            rows = pltpu.roll(rows, (128 + UNIT * k - offset) % 128, 1)
            joined = rows if joined is None else jnp.where(lane == k, rows, joined)
        pieces.append(joined)
    return jnp.concatenate(pieces, 1)


def filled(samples_ref):
    def step(index, seen):
        return jnp.maximum(seen, jnp.abs(samples_ref[index].astype(jnp.float32)))

    seen = lax.fori_loop(0, SOURCES, step, jnp.zeros((16, 128), jnp.float32), unroll=8)
    row = lax.broadcasted_iota(jnp.int32, (16, 128), 0)
    seen = jnp.max(jnp.where(row % 8 < 4, seen, 0.0), axis=0, keepdims=True)
    seen = jnp.broadcast_to(seen, (8, 128))
    for shift in (8, 4, 2, 1):
        seen = jnp.maximum(seen, pltpu.roll(seen, shift, 1))
    lane = lax.broadcasted_iota(jnp.int32, (8, 128), 1)
    place = lax.broadcasted_iota(jnp.int32, (8, 128), 0)
    hit = (seen > 0.0) & (lane == place * UNIT + UNIT - 1)
    return jnp.sum(jnp.where(hit, (1 << place).astype(jnp.float32), 0.0)).astype(jnp.int32)


def grid_kernel(last, samples_ref, table_ref, *refs):
    if last:
        carry_ref, out_ref, pair_ref, dense_ref, acc_ref, list_ref = refs
    else:
        out_ref, carried_ref, pair_ref, dense_ref, acc_ref, list_ref = refs
    bits = filled(samples_ref)
    count = jnp.int32(0)
    for place in range(128 // UNIT):
        list_ref[count] = place
        count = count + ((bits >> place) & 1)
    acc_ref[...] = jnp.zeros(acc_ref.shape, jnp.float32)
    if last:
        acc_ref[PLANES : PLANES + EDGE] = carry_ref[...]
    y_tab = table_ref[: 2 * ROWS, :GY]

    def step(index, _):
        block = list_ref[index]
        for part in range(STEP):
            packed = gather(samples_ref, part * (LANES // UNIT), block * UNIT)
            build(packed, y_tab, pair_ref, dense_ref, part * LANES, LANES)
        for plane in range(SPAN):
            product = lax.dot_general(
                pair_ref[plane * PAIR : (plane + 1) * PAIR],
                dense_ref[...],
                (((1,), (1,)), ((), ())),
                preferred_element_type=jnp.float32,
            )
            here = 4 * (block // (CAP // UNIT)) + plane
            acc_ref[here] = acc_ref[here] + product
        return 0

    lax.fori_loop(0, count, step, 0)

    z_tab = table_ref[2 * ROWS :]
    if last:
        lines = transform_z(acc_ref[0:PLANES], z_tab)
        edge = transform_z(acc_ref[PLANES:], z_tab)
    else:
        lines = transform_z(acc_ref[EDGE : EDGE + PLANES], z_tab)
        carried_ref[...] = acc_ref[0:EDGE]
    for row in range(ROWS):
        owner = (row // 4) * 2 + row % 4 // 2
        here = slice(row % 2 * GZ, (row % 2 + 1) * GZ)
        for coil in range(COILS):
            line = lines[coil * ROWS + row]
            out_ref[owner, coil, :, here] = jnp.concatenate([line[:, :GZ], line[:, GZ:]], 0).astype(
                jnp.bfloat16
            )
        for pair in range(COILS // 2) if last else ():
            pieces = []
            for inner in range(2):
                line = edge[(2 * pair + inner) * ROWS + row]
                pieces += [line[:, :GZ], line[:, GZ:]]
            out_ref[owner, COILS + pair, :, here] = jnp.concatenate(pieces, 0).astype(jnp.bfloat16)


def grid_chunk(samples, table, chunk, carry=None):
    last = carry is not None
    tiles = COILS + (COILS // 2 if last else 0)
    flops = 2 * SPAN * PAIR * GZ * SOURCES * CAP * BLOCKS // CHUNKS
    edges = (EDGE, PAIR, GZ)
    in_specs = [
        pl.BlockSpec((SOURCES, 16, 128), lambda q: (0, 0, CHUNKS - 1 - chunk)),
        pl.BlockSpec((2 * ROWS + 2 * GZ, 2 * GZ), lambda q: (0, 0)),
    ]
    out_specs = [pl.BlockSpec((GROUPS, tiles, 16, 2 * GZ), lambda q: (0, 0, 0, 0))]
    out_shape = [jax.ShapeDtypeStruct((GROUPS, tiles, 16, 2 * GZ), jnp.bfloat16)]
    operands = [samples, table]
    if last:
        in_specs.append(pl.BlockSpec(edges, lambda q: (0, 0, 0)))
        operands.append(carry)
    else:
        out_specs.append(pl.BlockSpec(edges, lambda q: (0, 0, 0)))
        out_shape.append(jax.ShapeDtypeStruct(edges, jnp.float32))
    return pl.pallas_call(
        lambda *refs: grid_kernel(last, *refs),
        grid=(1,),
        in_specs=in_specs,
        out_specs=out_specs,
        out_shape=out_shape,
        scratch_shapes=[
            pltpu.VMEM((SPAN * PAIR, STEP * LANES), jnp.bfloat16),
            pltpu.VMEM((GZ, STEP * LANES), jnp.bfloat16),
            pltpu.VMEM((PLANES + EDGE + 1, PAIR, GZ), jnp.float32),
            pltpu.SMEM((9,), jnp.int32),
        ],
        compiler_params=pltpu.CompilerParams(vmem_limit_bytes=36 * 2**20),
        cost_estimate=pl.CostEstimate(flops=flops, bytes_accessed=4 * 2**20, transcendentals=0),
        name="grid_chunk",
    )(*operands)


def combine_kernel(first_ref, second_ref, table_ref, other_hbm, out_ref, other_ref, sems):
    fetch = pltpu.make_async_copy(other_hbm, other_ref, sems.at[0])
    fetch.start()
    core = lax.axis_index("core")
    depth = GROUPS * 16

    def tables(index):
        rows, columns = 2 * GX * (index // 2), depth * (index % 2)
        return table_ref[rows : rows + 2 * GX, columns : columns + depth]

    def own(coil, part, lanes):
        rows = 4 * GX + (2 * coil + part) * GX
        return table_ref[rows : rows + GX, lanes]

    def other(coil, part, lanes):
        return other_ref[coil, part, :, lanes]

    for e in range(2):
        lanes = slice(e * GZ, (e + 1) * GZ)
        total = None
        for maps, pair in ((own, core), (other, 1 - core)):
            edge_rows = second_ref[:, COILS + pair, :, lanes].reshape(depth, GZ)
            for coil in range(2):
                image = jnp.dot(
                    tables(CHUNKS + coil), edge_rows, preferred_element_type=jnp.float32
                )
                for chunk, ref in enumerate((first_ref, second_ref)):
                    rows = ref[:, 2 * pair + coil, :, lanes].reshape(depth, GZ)
                    image = image + jnp.dot(tables(chunk), rows, preferred_element_type=jnp.float32)
                if maps is other and e == coil == 0:
                    fetch.wait()
                image_re, image_im = image[:GX], image[GX:]
                map_re = maps(coil, 0, lanes).astype(jnp.float32)
                map_im = maps(coil, 1, lanes).astype(jnp.float32)
                real = map_re * image_re + map_im * image_im
                imag = map_re * image_im - map_im * image_re
                total = [real, imag] if total is None else [total[0] + real, total[1] + imag]
        for part in range(2):
            out_ref[:, part, :, lanes] = total[part].astype(jnp.bfloat16).reshape(8, GX // 8, GZ)


def combine(first, second, table, other):
    vmem, hbm = pl.BlockSpec(memory_space=pltpu.VMEM), pl.BlockSpec(memory_space=pltpu.HBM)
    return pl.pallas_call(
        combine_kernel,
        in_specs=[vmem, vmem, vmem, hbm],
        out_specs=vmem,
        out_shape=jax.ShapeDtypeStruct((8, 2, GX // 8, 2 * GZ), jnp.bfloat16),
        scratch_shapes=[
            pltpu.VMEM((2, 2, GX, 2 * GZ), jnp.bfloat16),
            pltpu.SemaphoreType.DMA((1,)),
        ],
        compiler_params=pltpu.CompilerParams(vmem_limit_bytes=36 * 2**20),
        cost_estimate=pl.CostEstimate(
            flops=2 * 4 * 2 * GX * 3 * GROUPS * 16 * 2 * GZ,
            bytes_accessed=8 * 2**20,
            transcendentals=0,
        ),
        name="combine",
    )(first, second, table, other)


def add_kernel(parts_ref, out_ref):
    for half in range(2):
        total = parts_ref[half].astype(jnp.float32)
        for chip in range(1, 4):
            total = total + parts_ref[2 * chip + half].astype(jnp.float32)
        for e in range(2):
            for part in range(2):
                out_ref[part, :, 2 * half + e, :] = total[part, :, e * GZ : (e + 1) * GZ]


def add(parts):
    return pl.pallas_call(
        add_kernel,
        out_shape=jax.ShapeDtypeStruct((2, GX // 8, 4, GZ), jnp.float32),
        compiler_params=pltpu.CompilerParams(vmem_limit_bytes=16 * 2**20),
        name="add",
    )(parts)


def pack_kernel(values_ref, offsets_ref, cells_ref, slots_ref, out_ref):
    used = slots_ref[...] < SLOTS
    cells = cells_ref[...]
    values = [values_ref[coil].astype(jnp.float32) for coil in range(2)]
    rows = [jnp.where(used, values[r // 2][r % 2 : r % 2 + 1], 0.0) for r in range(4)]
    spots = (cells // (GY * GZ), cells // GZ % GY, cells % GZ)
    first = lax.axis_index("core") == 0
    for axis in range(3):
        offset = offsets_ref[axis : axis + 1].astype(jnp.float32)
        rows.append(jnp.where(first, offset, spots[axis].astype(jnp.float32)))
    rows.append(jnp.zeros((1, SLOTS), jnp.float32))
    packed = jnp.concatenate(rows, 0).astype(jnp.bfloat16)
    width = BLOCKS * CAP
    for group in range(GROUPS):
        part = packed[:, group * width : (group + 1) * width]
        for copy in range(ZH):
            out_ref[copy * GROUPS + group] = part


def pack(values, offsets, cells, slots):
    return pl.pallas_call(
        pack_kernel,
        out_shape=jax.ShapeDtypeStruct((ZH * GROUPS, 8, BLOCKS * CAP), jnp.bfloat16),
        compiler_params=pltpu.CompilerParams(vmem_limit_bytes=56 * 2**20),
        name="pack",
    )(values, offsets, cells.reshape(1, SLOTS), slots.reshape(1, SLOTS))


def turn(array, axes):
    return lax.all_to_all(array, axes, split_axis=0, concat_axis=0, tiled=True)


def body(sample_values, sample_offsets, sample_cells, sample_slots, sensitivity):
    packed = pack(sample_values, sample_offsets, sample_cells, sample_slots)
    packed, sensitivity = lax.optimization_barrier((packed, sensitivity))
    planes = ("zl", "x", "core")
    got = turn(packed, ("zh",) + planes)
    samples = got.reshape(SOURCES, 16, BLOCKS * CAP)

    def pick(tables, axis):
        here = lax.axis_index(axis)
        return lax.dynamic_index_in_dim(jnp.asarray(tables), here, 0, keepdims=False)

    table = pick(grid_table(), "zh")
    core = lax.axis_index("core")

    def maps(half):
        rows = lax.dynamic_slice_in_dim(sensitivity, 2 * half, 2, 3)
        return rows.reshape(2, 2, GX, 2 * GZ)

    other = lax.ppermute(maps(1 - core), "core", [(0, 1), (1, 0)])
    first, carry = grid_chunk(samples, table, 0)
    first = turn(first, planes)
    (second,) = grid_chunk(samples, table, 1, carry)
    pairs = x_tables().reshape(2, 2, 2 * GX, GROUPS * 16).transpose(0, 2, 1, 3)
    tables = jnp.asarray(pairs.reshape(4 * GX, 2 * GROUPS * 16))
    tables = jnp.concatenate([tables, maps(core).reshape(4 * GX, 2 * GZ)], 0)
    partial = combine(first, turn(second, planes), tables, other)
    return add(turn(partial, ("y", "core")))


def solution(mesh):
    fine = Mesh(mesh.devices.reshape(8, 2, 4, 4, 2), ("zh", "zl", "x", "y", "core"))
    space, coil = ("zh", "zl", "x"), ("y", "core")
    placed = (
        P(coil, None, space),
        P(None, space),
        P(space),
        P(space),
        P(coil, None, None, space, None),
    )
    return jax.shard_map(
        body, mesh=fine, in_specs=placed, out_specs=P(None, coil, space, None), check_vma=False
    )
```

```python
import math

import jax
import jax.numpy as jnp
import ml_dtypes
import numpy as np
from jax import lax
from jax.experimental import pallas as pl
from jax.experimental.pallas import tpu as pltpu
from jax.sharding import Mesh
from jax.sharding import PartitionSpec as P

GX = 256
GY = 256
GZ = 256
SLOTS = 4096
CAP = 64

BETA = 9.0
TERMS = 31

ZH = 8
SOURCES = 64
UNIT = 16
GROUPS = 16
BLOCKS = 4
LANES = 256
STEP = 4
COILS = 4
ROWS = 32
TAPS = 4
SPAN = 7
PAIR = 2 * COILS * ROWS
HALF = PAIR // 2
CHUNKS = 2
PLANES = 8
EDGE = 3


def series():
    quarter = 0.25 * BETA * BETA
    terms = [quarter**k / float(math.factorial(k)) ** 2 for k in range(TERMS)]
    total = math.fsum(terms)
    return [float(np.float32(t / total)) for t in terms]


def waves():
    counter = np.arange(256)
    phase = (counter[:, None] * counter[None, :] % 256).astype(np.float32) * np.float32(
        2.0 * math.pi / 256
    )
    scale = np.float32(1.0 / 16.0)
    both = np.stack([np.cos(phase) * scale, np.sin(phase) * scale], 0)
    return both.astype(ml_dtypes.bfloat16).astype(np.float32)


def z_table():
    cosine, sine = waves()
    return np.block([[cosine, sine], [-sine, cosine]]).astype(ml_dtypes.bfloat16)


def y_table():
    both = waves().reshape(2, ZH, ROWS, 256)
    return both.transpose(1, 0, 2, 3).reshape(ZH, 2 * ROWS, 256).astype(ml_dtypes.bfloat16)


def grid_table():
    rows = np.zeros((ZH, 2 * ROWS, 2 * GZ), ml_dtypes.bfloat16)
    rows[:, :, :GY] = y_table()
    return np.concatenate([rows, np.broadcast_to(z_table(), (ZH, 2 * GZ, 2 * GZ))], 1)


def x_columns(planes, part):
    cosine, sine = waves()
    if part == 0:
        return np.concatenate([cosine[:, planes], sine[:, planes]], 0)
    return np.concatenate([-sine[:, planes], cosine[:, planes]], 0)


def x_tables():
    main = []
    for first in (PLANES + EDGE, 0):
        cols = []
        for group in range(GROUPS):
            planes = (16 * group + first + np.arange(PLANES) - 1) % GX
            cols += [x_columns(planes, 0), x_columns(planes, 1)]
        main.append(np.concatenate(cols, 1))
    edge = []
    for coil in range(2):
        cols = []
        for group in range(GROUPS):
            planes = (16 * group + PLANES + np.arange(EDGE + 1) - 1) % GX
            real = np.arange(EDGE + 1) < EDGE
            for other in range(2):
                keep = real & (other == coil)
                cols += [x_columns(planes, part) * keep for part in range(2)]
        edge.append(np.concatenate(cols, 1))
    return np.stack(main + edge).astype(ml_dtypes.bfloat16)


def tap_rows(first, second, lanes):
    row = lax.broadcasted_iota(jnp.int32, (8, lanes), 0)
    offset = jnp.where(row < TAPS, first, second)
    distance = offset + (1.0 - (row % TAPS).astype(jnp.float32))
    inner = jnp.maximum(1.0 - 0.25 * distance * distance, 0.0)
    coefficients = series()
    total = jnp.full((8, lanes), coefficients[-1], jnp.float32)
    for value in coefficients[-2::-1]:
        total = total * inner + value
    return total


def dense_rows(weights, base, lanes):
    high = base // 16
    low = base % 16
    row = lax.broadcasted_iota(jnp.int32, (16, lanes), 0)
    pattern = jnp.zeros((16, lanes), jnp.float32)
    for tap in range(TAPS):
        pattern = jnp.where(row == (low + tap) % 16, weights[tap], pattern)
    place = jnp.where(row < low, (high + 1) % 16, high).astype(jnp.float32)
    pattern = pattern.astype(jnp.bfloat16)
    place = place.astype(jnp.bfloat16)
    zero = jnp.zeros((16, lanes), jnp.bfloat16)
    return [
        jnp.where(place == jnp.bfloat16(block), pattern, zero) for block in range(16)
    ]


def build(packed, y_tab, pair_ref, dense_ref, at, lanes):
    taps_xy = tap_rows(packed[4:5], packed[5:6], lanes)
    taps_z = tap_rows(packed[6:7], packed[6:7], lanes)
    cell = packed.astype(jnp.int32)
    base_x = cell[12:13]
    base_y = (cell[13:14] + 255) % 256
    base_z = (cell[14:15] + 255) % 256
    z_blocks = dense_rows([taps_z[t : t + 1] for t in range(TAPS)], base_z, lanes)
    for block in range(16):
        dense_ref[block * 16 : (block + 1) * 16, at : at + lanes] = z_blocks[block]
    y_blocks = dense_rows([taps_xy[4 + t : 5 + t] for t in range(TAPS)], base_y, lanes)
    turn = jnp.dot(y_tab, jnp.concatenate(y_blocks, 0), preferred_element_type=jnp.float32)
    turn_re, turn_im = turn[:ROWS], turn[ROWS:]
    real, imag = [], []
    for coil in range(COILS):
        row = (coil // 2) * 8 + (coil % 2) * 2
        value_re, value_im = packed[row : row + 1], packed[row + 1 : row + 2]
        real.append(value_re * turn_re - value_im * turn_im)
        imag.append(value_re * turn_im + value_im * turn_re)
    values = real + imag
    row = lax.broadcasted_iota(jnp.int32, (8, lanes), 0)
    dense_x = jnp.zeros((8, lanes), jnp.float32)
    for tap in range(TAPS):
        dense_x = jnp.where(row == base_x + tap, taps_xy[tap : tap + 1], dense_x)
    for plane in range(SPAN):
        weight = dense_x[plane : plane + 1]
        for part in range(2 * COILS):
            start = plane * PAIR + part * ROWS
            pair_ref[start : start + ROWS, at : at + lanes] = (values[part] * weight).astype(
                jnp.bfloat16
            )


def transform_z(grid_planes, z_tab):
    planes = grid_planes.shape[0]
    grid = grid_planes.astype(jnp.bfloat16)
    joined = jnp.concatenate([grid[:, :HALF], grid[:, HALF:]], axis=2)
    along = jnp.dot(
        joined.reshape(planes * HALF, 2 * GZ), z_tab, preferred_element_type=jnp.float32
    )
    return jnp.swapaxes(along.reshape(planes, HALF, 2 * GZ), 0, 1)


def gather(samples_ref, start, offset, lanes):
    per = 128 // UNIT
    lane = lax.broadcasted_iota(jnp.int32, (16, 128), 1) // UNIT
    pieces = []
    for piece in range(LANES // 128):
        joined = None
        for k in range(per):
            rows = samples_ref[start + piece * per + k, :, lanes].astype(jnp.float32)
            rows = pltpu.roll(rows, (128 + UNIT * k - offset) % 128, 1)
            joined = rows if joined is None else jnp.where(lane == k, rows, joined)
        pieces.append(joined)
    return jnp.concatenate(pieces, 1)


def filled(samples_ref, lanes):
    def step(index, seen):
        return jnp.maximum(seen, jnp.abs(samples_ref[index, :, lanes].astype(jnp.float32)))

    seen = lax.fori_loop(0, SOURCES, step, jnp.zeros((16, 128), jnp.float32), unroll=8)
    row = lax.broadcasted_iota(jnp.int32, (16, 128), 0)
    seen = jnp.max(jnp.where(row % 8 < 4, seen, 0.0), axis=0, keepdims=True)
    seen = jnp.broadcast_to(seen, (8, 128))
    for shift in (8, 4, 2, 1):
        seen = jnp.maximum(seen, pltpu.roll(seen, shift, 1))
    lane = lax.broadcasted_iota(jnp.int32, (8, 128), 1)
    place = lax.broadcasted_iota(jnp.int32, (8, 128), 0)
    hit = (seen > 0.0) & (lane == place * UNIT + UNIT - 1)
    return jnp.sum(jnp.where(hit, (1 << place).astype(jnp.float32), 0.0)).astype(jnp.int32)


def grid_kernel(last, samples_ref, table_ref, *refs):
    if last:
        carry_ref, out_ref, pair_ref, dense_ref, acc_ref, list_ref = refs
    else:
        out_ref, carried_ref, pair_ref, dense_ref, acc_ref, list_ref = refs
    first = 0 if last else 128
    lanes = slice(first, first + 128)
    bits = filled(samples_ref, lanes)
    count = jnp.int32(0)
    for place in range(128 // UNIT):
        list_ref[count] = place
        count = count + ((bits >> place) & 1)
    acc_ref[...] = jnp.zeros(acc_ref.shape, jnp.float32)
    if last:
        acc_ref[PLANES : PLANES + EDGE] = carry_ref[...]
    y_tab = table_ref[: 2 * ROWS, :GY]

    def step(index, _):
        block = list_ref[index]
        for part in range(STEP):
            packed = gather(samples_ref, part * (LANES // UNIT), block * UNIT, lanes)
            build(packed, y_tab, pair_ref, dense_ref, part * LANES, LANES)
        for plane in range(SPAN):
            product = lax.dot_general(
                pair_ref[plane * PAIR : (plane + 1) * PAIR],
                dense_ref[...],
                (((1,), (1,)), ((), ())),
                preferred_element_type=jnp.float32,
            )
            here = 4 * (block // (CAP // UNIT)) + plane
            acc_ref[here] = acc_ref[here] + product
        return 0

    lax.fori_loop(0, count, step, 0)

    z_tab = table_ref[2 * ROWS :]
    if last:
        lines = transform_z(acc_ref[0:PLANES], z_tab)
        edge = transform_z(acc_ref[PLANES:], z_tab)
    else:
        lines = transform_z(acc_ref[EDGE : EDGE + PLANES], z_tab)
        carried_ref[...] = acc_ref[0:EDGE]
    for row in range(ROWS):
        owner = (row // 4) * 2 + row % 4 // 2
        here = slice(row % 2 * GZ, (row % 2 + 1) * GZ)
        for coil in range(COILS):
            line = lines[coil * ROWS + row]
            out_ref[owner, coil, :, here] = jnp.concatenate([line[:, :GZ], line[:, GZ:]], 0).astype(
                jnp.bfloat16
            )
        for pair in range(COILS // 2) if last else ():
            pieces = []
            for inner in range(2):
                line = edge[(2 * pair + inner) * ROWS + row]
                pieces += [line[:, :GZ], line[:, GZ:]]
            out_ref[owner, COILS + pair, :, here] = jnp.concatenate(pieces, 0).astype(jnp.bfloat16)


def grid_chunk(samples, table, chunk, carry=None):
    last = carry is not None
    tiles = COILS + (COILS // 2 if last else 0)
    flops = 2 * SPAN * PAIR * GZ * SOURCES * CAP * BLOCKS // CHUNKS
    edges = (EDGE, PAIR, GZ)
    vmem = pl.BlockSpec(memory_space=pltpu.VMEM)
    in_specs = [vmem, vmem]
    out_specs = [vmem]
    out_shape = [jax.ShapeDtypeStruct((GROUPS, tiles, 16, 2 * GZ), jnp.bfloat16)]
    operands = [samples, table]
    if last:
        in_specs.append(vmem)
        operands.append(carry)
    else:
        out_specs.append(vmem)
        out_shape.append(jax.ShapeDtypeStruct(edges, jnp.float32))
    return pl.pallas_call(
        lambda *refs: grid_kernel(last, *refs),
        in_specs=in_specs,
        out_specs=out_specs,
        out_shape=out_shape,
        scratch_shapes=[
            pltpu.VMEM((SPAN * PAIR, STEP * LANES), jnp.bfloat16),
            pltpu.VMEM((GZ, STEP * LANES), jnp.bfloat16),
            pltpu.VMEM((PLANES + EDGE + 1, PAIR, GZ), jnp.float32),
            pltpu.SMEM((9,), jnp.int32),
        ],
        compiler_params=pltpu.CompilerParams(vmem_limit_bytes=36 * 2**20),
        cost_estimate=pl.CostEstimate(flops=flops, bytes_accessed=4 * 2**20, transcendentals=0),
        name="grid_chunk",
    )(*operands)


def combine_kernel(first_ref, second_ref, table_ref, other_hbm, out_ref, other_ref, sems):
    fetch = pltpu.make_async_copy(other_hbm, other_ref, sems.at[0])
    fetch.start()
    core = lax.axis_index("core")
    depth = GROUPS * 16

    def tables(index):
        rows, columns = 2 * GX * (index // 2), depth * (index % 2)
        return table_ref[rows : rows + 2 * GX, columns : columns + depth]

    def own(coil, part, lanes):
        rows = 4 * GX + (2 * coil + part) * GX
        return table_ref[rows : rows + GX, lanes]

    def other(coil, part, lanes):
        return other_ref[coil, part, :, lanes]

    for e in range(2):
        lanes = slice(e * GZ, (e + 1) * GZ)
        total = None
        for maps, pair in ((own, core), (other, 1 - core)):
            edge_rows = second_ref[:, COILS + pair, :, lanes].reshape(depth, GZ)
            for coil in range(2):
                image = jnp.dot(
                    tables(CHUNKS + coil), edge_rows, preferred_element_type=jnp.float32
                )
                for chunk, ref in enumerate((first_ref, second_ref)):
                    rows = ref[:, 2 * pair + coil, :, lanes].reshape(depth, GZ)
                    image = image + jnp.dot(tables(chunk), rows, preferred_element_type=jnp.float32)
                if maps is other and e == coil == 0:
                    fetch.wait()
                image_re, image_im = image[:GX], image[GX:]
                map_re = maps(coil, 0, lanes).astype(jnp.float32)
                map_im = maps(coil, 1, lanes).astype(jnp.float32)
                real = map_re * image_re + map_im * image_im
                imag = map_re * image_im - map_im * image_re
                total = [real, imag] if total is None else [total[0] + real, total[1] + imag]
        for part in range(2):
            out_ref[:, part, :, lanes] = total[part].astype(jnp.bfloat16).reshape(8, GX // 8, GZ)


def combine(first, second, table, other):
    vmem, hbm = pl.BlockSpec(memory_space=pltpu.VMEM), pl.BlockSpec(memory_space=pltpu.HBM)
    return pl.pallas_call(
        combine_kernel,
        in_specs=[vmem, vmem, vmem, hbm],
        out_specs=vmem,
        out_shape=jax.ShapeDtypeStruct((8, 2, GX // 8, 2 * GZ), jnp.bfloat16),
        scratch_shapes=[
            pltpu.VMEM((2, 2, GX, 2 * GZ), jnp.bfloat16),
            pltpu.SemaphoreType.DMA((1,)),
        ],
        compiler_params=pltpu.CompilerParams(vmem_limit_bytes=36 * 2**20),
        cost_estimate=pl.CostEstimate(
            flops=2 * 4 * 2 * GX * 3 * GROUPS * 16 * 2 * GZ,
            bytes_accessed=8 * 2**20,
            transcendentals=0,
        ),
        name="combine",
    )(first, second, table, other)


def add_kernel(parts_ref, out_ref):
    for half in range(2):
        total = parts_ref[half].astype(jnp.float32)
        for chip in range(1, 4):
            total = total + parts_ref[2 * chip + half].astype(jnp.float32)
        for e in range(2):
            for part in range(2):
                out_ref[part, :, 2 * half + e, :] = total[part, :, e * GZ : (e + 1) * GZ]


def add(parts):
    return pl.pallas_call(
        add_kernel,
        out_shape=jax.ShapeDtypeStruct((2, GX // 8, 4, GZ), jnp.float32),
        compiler_params=pltpu.CompilerParams(vmem_limit_bytes=16 * 2**20),
        name="add",
    )(parts)


def pack_kernel(values_ref, offsets_ref, cells_ref, slots_ref, out_ref):
    used = slots_ref[...] < SLOTS
    cells = cells_ref[...]
    values = [values_ref[coil].astype(jnp.float32) for coil in range(2)]
    rows = [jnp.where(used, values[r // 2][r % 2 : r % 2 + 1], 0.0) for r in range(4)]
    spots = (cells // (GY * GZ), cells // GZ % GY, cells % GZ)
    first = lax.axis_index("core") == 0
    for axis in range(3):
        offset = offsets_ref[axis : axis + 1].astype(jnp.float32)
        rows.append(jnp.where(first, offset, spots[axis].astype(jnp.float32)))
    rows.append(jnp.zeros((1, SLOTS), jnp.float32))
    packed = jnp.concatenate(rows, 0).astype(jnp.bfloat16)
    width = BLOCKS * CAP
    for group in range(GROUPS):
        part = packed[:, group * width : (group + 1) * width]
        for copy in range(ZH):
            out_ref[copy * GROUPS + group] = part


def pack(values, offsets, cells, slots):
    return pl.pallas_call(
        pack_kernel,
        out_shape=jax.ShapeDtypeStruct((ZH * GROUPS, 8, BLOCKS * CAP), jnp.bfloat16),
        compiler_params=pltpu.CompilerParams(vmem_limit_bytes=56 * 2**20),
        name="pack",
    )(values, offsets, cells.reshape(1, SLOTS), slots.reshape(1, SLOTS))


def turn(array, axes):
    return lax.all_to_all(array, axes, split_axis=0, concat_axis=0, tiled=True)


def body(sample_values, sample_offsets, sample_cells, sample_slots, sensitivity):
    packed = pack(sample_values, sample_offsets, sample_cells, sample_slots)
    packed, sensitivity = lax.optimization_barrier((packed, sensitivity))
    planes = ("zl", "x", "core")
    got = turn(packed, ("zh",) + planes)
    samples = got.reshape(SOURCES, 16, BLOCKS * CAP)

    def pick(tables, axis):
        here = lax.axis_index(axis)
        return lax.dynamic_index_in_dim(jnp.asarray(tables), here, 0, keepdims=False)

    table = pick(grid_table(), "zh")
    core = lax.axis_index("core")

    def maps(half):
        rows = lax.dynamic_slice_in_dim(sensitivity, 2 * half, 2, 3)
        return rows.reshape(2, 2, GX, 2 * GZ)

    other = lax.ppermute(maps(1 - core), "core", [(0, 1), (1, 0)])
    first, carry = grid_chunk(samples, table, 0)
    first = turn(first, planes)
    (second,) = grid_chunk(samples, table, 1, carry)
    pairs = x_tables().reshape(2, 2, 2 * GX, GROUPS * 16).transpose(0, 2, 1, 3)
    tables = jnp.asarray(pairs.reshape(4 * GX, 2 * GROUPS * 16))
    tables = jnp.concatenate([tables, maps(core).reshape(4 * GX, 2 * GZ)], 0)
    partial = combine(first, turn(second, planes), tables, other)
    return add(turn(partial, ("y", "core")))


def solution(mesh):
    fine = Mesh(mesh.devices.reshape(8, 2, 4, 4, 2), ("zh", "zl", "x", "y", "core"))
    space, coil = ("zh", "zl", "x"), ("y", "core")
    placed = (
        P(coil, None, space),
        P(None, space),
        P(space),
        P(space),
        P(coil, None, None, space, None),
    )
    return jax.shard_map(
        body, mesh=fine, in_specs=placed, out_specs=P(None, coil, space, None), check_vma=False
    )
```
